128 devices in a mesh: section: 8 (over z, x_lo), tensor: 16 (over x_hi, y, core).
Axes of the slice: x: 4 (x_hi: 2, x_lo: 2; x = x_hi * 2 + x_lo), y: 4, z: 4, core: 2. Of those that a mesh axis runs over, the one named last changes fastest.
Arguments:
- state: bfloat16 [8, 2048, 5120], P('section', 'tensor'), may hold values from -6 to 6
- docs: int32 [8, 2048], P('section', 'tensor'), may hold values from 0 to 15, never falling along the last dimension, each value on 1 to 512 neighbouring positions
- gain: float32 [8, 5120], P('section'), may hold values from 0.25 to 1.75
- w_query: bfloat16 [8, 5120, 4096], P('section', None, 'tensor'), may hold values from -1 to 1
- w_keyval: bfloat16 [8, 5120, 2048], P('section', None, 'tensor'), may hold values from -1 to 1
- w_out: bfloat16 [8, 4096, 5120], P('section', 'tensor'), may hold values from -0.09375 to 0.09375
Outputs:
- next_state: bfloat16 [8, 2048, 5120], P('section', 'tensor')
- next_docs: int32 [8, 2048], P('section', 'tensor')
The draws below stay inside these ranges and needn't reach their ends.
Inputs may be any that keep to these rules, and one draw needn't show every extreme that they name: `docs`: in each layer's row the ids never fall; each document holds 1 to 512 tokens and one holds exactly 512.
All inputs are finite; a program needn't handle non-finite values.
Results may differ from the reference program's by a relative error of at most 0.014.
Values may be sent and summed in bfloat16 or wider, within the bound.
A program may use at most 128 MiB of HBM per device.

```python
import math
import jax
import jax.numpy as jnp
import numpy as np
from jax import lax

D = 5120
HEAD_DIM = 128
QH_DEV = 2
HEADS = 32
KV_HEADS = 8
TOKENS = 2048
N_SECTION = 8
N_TENSOR = 16


def draw_state(key, part):
    own_key = jax.random.fold_in(key, 11)
    noise = jax.random.truncated_normal(jax.random.fold_in(own_key, 1), -6.0, 6.0, (N_SECTION, TOKENS, D), jnp.float32)
    values = noise
    return values.astype(jnp.bfloat16)


def draw_w_query(key, part):
    own_key = jax.random.fold_in(key, 12)
    width = HEADS * HEAD_DIM
    values = jax.random.truncated_normal(own_key, -6.0, 6.0, (N_SECTION, D, width), jnp.float32) * D ** (-0.5)
    return values.astype(jnp.bfloat16)


def draw_w_keyval(key, part):
    own_key = jax.random.fold_in(key, 13)
    width = 2 * KV_HEADS * HEAD_DIM
    values = jax.random.truncated_normal(own_key, -6.0, 6.0, (N_SECTION, D, width), jnp.float32) * D ** (-0.5)
    return values.astype(jnp.bfloat16)


def levels(key, dims, pieces, smallest, high):
    def one(axis_at, blocks):
        draws = jax.random.uniform(jax.random.fold_in(jax.random.fold_in(key, 6), axis_at), (blocks,), jnp.float32, smallest / len(pieces), high / len(pieces))
        return jnp.repeat(jnp.exp(draws), dims[axis_at] // blocks).reshape((-1,) + (1,) * (len(dims) - axis_at - 1))

    factor_of = one(*pieces[0])
    for cut in pieces[1:]:
        factor_of = factor_of * one(*cut)
    return factor_of


def split_up(amount, total, limit, slope):
    portions = [(1 << 20) // math.isqrt(grade ** slope) + 1 for grade in range(2, amount + 1)]
    spare, holding = total - limit - (amount - 1), [1] * (amount - 1)
    while spare > 0:
        candidates = [i for i in range(amount - 1) if holding[i] < limit]
        pool, remaining = sum([portions[i] for i in candidates]), spare
        for i in candidates:
            addition = min(limit - holding[i], max(1, remaining * portions[i] // pool), spare)
            holding[i] = holding[i] + addition
            spare = spare - addition
    return np.array([limit] + holding)


def ragged(rng, count, total, limit, slope):
    if count == 2:
        one = jax.random.randint(rng, (), max(1, total - limit), min(limit, total - 1) + 1)
        return jnp.stack([one, total - one])
    lengths = jnp.asarray(split_up(count, total, limit, slope), jnp.int32)
    couples = (count - 1) // 2
    giver, receiver = lengths[1:1 + 2 * couples:2], lengths[2:2 + 2 * couples:2]
    margin = jnp.minimum(giver - 1, limit - receiver)
    moved = jax.random.randint(jax.random.fold_in(rng, 1), (couples,), 0, 1 << 20) % (margin + 1)
    lengths = lengths.at[1:1 + 2 * couples:2].set(giver - moved).at[2:2 + 2 * couples:2].set(receiver + moved)
    return lengths[jax.random.permutation(jax.random.fold_in(rng, 2), count)]


def bell_draw(stream_key, dims, scale, bound, pieces=(), kind=jnp.bfloat16):
    values = scale * jax.random.normal(stream_key, dims, jnp.float32)
    if pieces:
        values = values * levels(stream_key, dims, pieces, -0.22, 0.18)
    return jnp.clip(values, -bound, bound).astype(kind)


def setup_inputs(seed: int = 0) -> dict:
    key_list = jax.random.split(jax.random.key(seed), 7)
    state = draw_state(jax.random.fold_in(key_list[6], 71), 0)
    docs = jax.vmap(lambda own: jnp.searchsorted(jnp.cumsum(ragged(own, 16, TOKENS, TOKENS // 4, 1)), jnp.arange(TOKENS), side="right"))(jax.random.split(key_list[1], N_SECTION)).reshape((N_SECTION, TOKENS)).astype(jnp.int32)
    gain = jnp.clip(1.0 + 0.15 * jax.random.normal(key_list[2], (N_SECTION, D), jnp.float32), 0.25, 1.75)
    w_query = draw_w_query(jax.random.fold_in(key_list[6], 71), 0)
    w_keyval = draw_w_keyval(jax.random.fold_in(key_list[6], 71), 0)
    w_out = bell_draw(key_list[5], (N_SECTION, HEADS * HEAD_DIM, D), (HEADS * HEAD_DIM) ** -0.5, 0.09375, ((0, 8), (1, 16)))
    return dict(state=state, docs=docs, gain=gain, w_query=w_query, w_keyval=w_keyval, w_out=w_out)


def norm_tokens(values_in, gain_row):
    widened = values_in.astype(jnp.float32)
    factor = lax.rsqrt(lax.optimization_barrier(jnp.mean(widened * widened, axis=-1, keepdims=True)) + 1e-05)
    return (widened * factor * gain_row.astype(jnp.float32)).astype(jnp.bfloat16)

def attend(query_rows, key_rows, value_rows, doc_ids, first_row):
    count = query_rows.shape[0]
    length = key_rows.shape[0]
    scores = jnp.dot(query_rows, key_rows.T, preferred_element_type=jnp.float32) * key_rows.shape[1] ** (-0.5)
    row_pos = first_row + lax.iota(jnp.int32, count)
    col_pos = lax.iota(jnp.int32, length)
    query_docs = lax.dynamic_slice_in_dim(doc_ids, first_row, count, 0)
    visible = (col_pos[None, :] <= row_pos[:, None]) & (doc_ids[None, :length] == query_docs[:, None])
    scores = jnp.where(visible, scores, -jnp.inf)
    highest = lax.optimization_barrier(jnp.max(scores, axis=-1, keepdims=True))
    expo = jnp.exp(scores - highest)
    probs = (expo / lax.optimization_barrier(jnp.sum(expo, axis=-1, keepdims=True))).astype(jnp.bfloat16)
    return jnp.dot(probs, value_rows, preferred_element_type=jnp.float32).astype(jnp.bfloat16)

def section_layer(layer_args):
    layer_state, layer_docs, layer_gain, query_weight, keyval_weight, out_weight = layer_args
    normed = norm_tokens(layer_state, layer_gain)
    query = jnp.dot(normed, query_weight, preferred_element_type=jnp.float32).astype(jnp.bfloat16)
    keyval = jnp.dot(normed, keyval_weight, preferred_element_type=jnp.float32).astype(jnp.bfloat16)
    paired = keyval.reshape(TOKENS, KV_HEADS, 2, HEAD_DIM)
    all_keys = paired[:, :, 0, :]
    all_values = paired[:, :, 1, :]
    block_size = min(512, TOKENS)
    ratio = HEADS // KV_HEADS

    def one_head(head_index):
        head_query = lax.dynamic_slice_in_dim(query, head_index * HEAD_DIM, HEAD_DIM, 1)
        group_index = head_index // ratio
        head_keys = lax.dynamic_index_in_dim(all_keys, group_index, 1, keepdims=False)
        head_values = lax.dynamic_index_in_dim(all_values, group_index, 1, keepdims=False)

        def one_block(block_index):
            first_row = block_index * block_size
            block_rows = lax.dynamic_slice_in_dim(head_query, first_row, block_size, 0)
            return attend(block_rows, head_keys, head_values, layer_docs, first_row)
        outputs = lax.map(one_block, jnp.arange(TOKENS // block_size, dtype=jnp.int32))
        return outputs.reshape(TOKENS, HEAD_DIM)
    heads_out = lax.map(one_head, jnp.arange(HEADS, dtype=jnp.int32))
    attended = jnp.transpose(heads_out, (1, 0, 2)).reshape(TOKENS, HEADS * HEAD_DIM)
    groups = jnp.transpose(attended.reshape(TOKENS, N_TENSOR, QH_DEV * HEAD_DIM), (1, 0, 2))
    weight_groups = out_weight.reshape(N_TENSOR, QH_DEV * HEAD_DIM, D)

    def add_group(running, pair):
        partial_term = jnp.dot(pair[0], pair[1], preferred_element_type=jnp.float32).astype(jnp.bfloat16)
        partial_term = lax.optimization_barrier(partial_term)
        return (running + partial_term.astype(jnp.float32), None)
    delta, _ = lax.scan(add_group, jnp.zeros((TOKENS, D), jnp.float32), (groups, weight_groups))
    return (layer_state.astype(jnp.float32) + delta).astype(jnp.bfloat16)

def reference(state, docs, gain, w_query, w_keyval, w_out):
    layer_out = lax.map(section_layer, (state, docs, gain, w_query, w_keyval, w_out))
    next_state = jnp.roll(layer_out, 1, axis=0)
    next_docs = jnp.roll(docs, 1, axis=0)
    return (next_state, next_docs)
```

```python
import functools

import jax
import jax.numpy as jnp
from jax import lax
from jax.experimental import pallas as pl
from jax.experimental.pallas import tpu as pltpu
from jax.sharding import PartitionSpec as P

MESH = pl.DeviceIdType.MESH
BLK = 128
HALF = 64
HD = 128
WIN = 5
PAD = WIN - 1
YS = 4
NJ = 10
NW = 5
SLOTS = ((0, 0), (1, 0), (0, 3), (0, 1), (1, 3), (1, 1), (0, 2), (1, 2))
OWN, ACROSS, BEHIND, AHEAD, BEHIND2, AHEAD2, FAR, FAR2 = range(8)
LOG2E = 1.4426950408889634
FIRST = pl.ds(0, HALF)
SECOND = pl.ds(HALF, HALF)


def body(
    state_ref, docs_ref, gain_ref, wq_ref, wkv_ref, wo_ref,
    out_ref, odocs_ref,
    state, gain, xg, w, wo, q, kv, dc, att, att_out,
    far, fwd, bwd, mine, half_f, half_b, got_f, got_b, done,
    load_sem, xs_sem, xr_sem, dsend, drecv, ws_sem, wr_sem, kvs_sem, kvr_sem,
    wos_sem, wor_sem, ats_sem, atr_sem, rs_send, rs_recv, sh_send, sh_recv,
):
    width = state.shape[1]
    cw = width // NJ
    ww = width // NW
    sec = lax.axis_index("section")
    ten = lax.axis_index("tensor")
    nsec = lax.axis_size("section")
    xh, y, core = ten // (2 * YS), (ten // 2) % YS, ten % 2

    def at(dh, dy, dcore=0):
        return (sec, ((xh + dh) % 2) * (2 * YS) + ((y + dy) % YS) * 2 + (core + dcore) % 2)

    def block_of(dh, dy):
        return ((xh + dh) % 2) * YS + (y + dy) % YS

    twin, across, ahead, behind = at(0, 0, 1), at(1, 0), at(0, 1), at(0, 3)
    following = ((sec + 1) % nsec, ten)
    before = ((sec + nsec - 1) % nsec, ten)

    loads = [
        pltpu.make_async_copy(state_ref.at[0], state, load_sem.at[0]),
        pltpu.make_async_copy(gain_ref, gain, load_sem.at[1]),
        pltpu.make_async_copy(docs_ref, dc.at[PAD + 2 * block_of(0, 0) + core], load_sem.at[2]),
        pltpu.make_async_copy(wq_ref.at[0], w.at[core], load_sem.at[3]),
        pltpu.make_async_copy(
            wkv_ref.at[0], w.at[2, :, pl.ds(pl.multiple_of(core * HD, HD), HD)], load_sem.at[4]
        ),
        pltpu.make_async_copy(
            wo_ref.at[0], wo.at[0, pl.ds(pl.multiple_of(core * 256, 256), 256), :], load_sem.at[5]
        ),
    ]
    for copy in loads:
        copy.start()

    barrier = pltpu.get_barrier_semaphore()
    for other in (twin, across, ahead, behind, following, before):
        pl.semaphore_signal(barrier, inc=1, device_id=other, device_id_type=MESH)

    for index in range(PAD):
        kv[index] = jnp.zeros((BLK, 2 * HD), jnp.bfloat16)
        dc[index] = jnp.full((1, BLK), -1, jnp.int32)

    def remote(src, dst, send, recv, target):
        return pltpu.make_async_remote_copy(
            src_ref=src, dst_ref=dst, send_sem=send, recv_sem=recv, device_id=target, device_id_type=MESH
        )

    sent = []

    def go(copy):
        copy.start()
        sent.append(copy)
        return copy

    def piece(number, src, dst, part, target):
        rows = FIRST if part == 0 else SECOND
        return remote(
            xg.at[src, rows, :], xg.at[dst, rows, :], xs_sem.at[number], xr_sem.at[dst, part], target
        )

    def arrived(slot, part):
        rows = FIRST if part == 0 else SECOND
        remote(
            xg.at[slot, rows, :], xg.at[slot, rows, :], xs_sem.at[0], xr_sem.at[slot, part], twin
        ).wait_recv()

    def doc_pair(dh, dy):
        return dc.at[pl.ds(PAD + 2 * block_of(dh, dy), 2)]

    def send_docs(number, dh, dy, recv, target):
        ref = doc_pair(dh, dy)
        return remote(ref, ref, dsend.at[number], drecv.at[recv], target)

    def docs_arrived(recv, dh, dy):
        ref = doc_pair(dh, dy)
        remote(ref, ref, dsend.at[0], drecv.at[recv], twin).wait_recv()

    loads[0].wait()
    loads[1].wait()

    def norm(rows):
        wide = state[rows, :].astype(jnp.float32)
        factor = lax.rsqrt(jnp.mean(wide * wide, axis=-1, keepdims=True) + 1e-05)
        xg[OWN, rows, :] = (wide * factor * gain[...]).astype(jnp.bfloat16)

    norm(FIRST)
    pl.semaphore_wait(barrier, 6)
    go(piece(0, OWN, BEHIND, 0, ahead))
    go(piece(1, OWN, ACROSS, 0, across))
    norm(SECOND)
    go(piece(2, OWN, AHEAD, 1, behind))
    go(piece(3, OWN, BEHIND, 1, ahead))
    go(piece(4, OWN, AHEAD, 0, behind))
    across_last = piece(5, OWN, ACROSS, 1, across)
    across_last.start()

    loads[2].wait()
    own_docs = dc.at[PAD + 2 * block_of(0, 0) + core]
    go(remote(own_docs, own_docs, dsend.at[0], drecv.at[0], twin))
    go(remote(docs_ref, odocs_ref, dsend.at[9], drecv.at[9], following))
    go(remote(wq_ref.at[0], w.at[core], ws_sem.at[0], wr_sem.at[0], twin))
    kv_cols = w.at[2, :, pl.ds(pl.multiple_of(core * HD, HD), HD)]
    go(remote(wkv_ref.at[0], kv_cols, ws_sem.at[1], wr_sem.at[1], twin))
    twin_docs = dc.at[PAD + 2 * block_of(0, 0) + 1 - core]
    remote(twin_docs, twin_docs, dsend.at[0], drecv.at[0], twin).wait_recv()
    go(send_docs(1, 0, 0, 1, across))
    go(send_docs(2, 0, 0, 2, ahead))
    go(send_docs(3, 0, 0, 3, behind))

    def project(slot, count):
        rows = xg[pl.ds(slot, count)].reshape(count * BLK, width)
        for index in range(3):
            res = jnp.dot(rows, w[index], preferred_element_type=jnp.float32).astype(jnp.bfloat16)
            for one in range(count):
                dh, dy = SLOTS[slot + one]
                part = res[one * BLK : (one + 1) * BLK]
                if index < 2:
                    q[dh * YS + dy, 2 * index] = part[:, :HD]
                    q[dh * YS + dy, 2 * index + 1] = part[:, HD:]
                else:
                    kv[PAD + 2 * block_of(dh, dy) + core] = part
        for one in range(count):
            dh, dy = SLOTS[slot + one]
            ref = kv.at[PAD + 2 * block_of(dh, dy) + core]
            go(remote(ref, ref, kvs_sem.at[slot + one], kvr_sem.at[slot + one], twin))

    def wo_piece(chunk):
        return pl.ds(chunk * ww, ww)

    def wo_across(chunk):
        dst = wo.at[1, pl.ds(pl.multiple_of(core * 256, 256), 256), wo_piece(chunk)]
        return remote(wo_ref.at[0, :, wo_piece(chunk)], dst, wos_sem.at[chunk], wor_sem.at[chunk], across)

    def wo_relay(chunk):
        ref = wo.at[1, pl.ds(pl.multiple_of(core * 256, 256), 256), wo_piece(chunk)]
        return remote(ref, ref, wos_sem.at[NW + chunk], wor_sem.at[NW + chunk], twin)

    def pass_wo(chunk):
        wo_across(chunk).wait_recv()
        go(wo_relay(chunk))

    arrived(BEHIND, 0)
    go(piece(6, BEHIND, FAR, 0, ahead))
    arrived(AHEAD, 1)
    go(piece(7, AHEAD, FAR, 1, behind))
    arrived(ACROSS, 0)
    go(piece(8, ACROSS, BEHIND2, 0, ahead))
    go(piece(10, ACROSS, AHEAD2, 0, behind))
    across_last.wait_send()
    for chunk in range(NW):
        go(wo_across(chunk))
    arrived(ACROSS, 1)
    go(piece(9, ACROSS, AHEAD2, 1, behind))
    go(piece(11, ACROSS, BEHIND2, 1, ahead))
    docs_arrived(1, 1, 0)
    go(send_docs(4, 1, 0, 4, ahead))
    go(send_docs(5, 1, 0, 5, behind))
    docs_arrived(2, 0, 3)
    go(send_docs(6, 0, 3, 6, ahead))
    docs_arrived(3, 0, 1)
    go(remote(
        wo_ref.at[0], wo.at[0, pl.ds(pl.multiple_of(core * 256, 256), 256), :],
        wos_sem.at[2 * NW], wor_sem.at[2 * NW], twin,
    ))

    for copy in loads[3:]:
        copy.wait()
    remote(w.at[1 - core], w.at[1 - core], ws_sem.at[0], wr_sem.at[0], twin).wait_recv()
    kv_cols2 = w.at[2, :, pl.ds(pl.multiple_of((1 - core) * HD, HD), HD)]
    remote(kv_cols2, kv_cols2, ws_sem.at[1], wr_sem.at[1], twin).wait_recv()
    project(OWN, 2)
    docs_arrived(4, 1, 3)
    go(send_docs(7, 1, 3, 7, ahead))
    docs_arrived(5, 1, 1)
    arrived(BEHIND, 1)
    arrived(AHEAD, 0)
    project(BEHIND, 2)
    pass_wo(0)
    arrived(BEHIND2, 0)
    go(piece(12, BEHIND2, FAR2, 0, ahead))
    arrived(AHEAD2, 1)
    go(piece(13, AHEAD2, FAR2, 1, behind))
    pass_wo(1)
    arrived(FAR, 0)
    arrived(FAR, 1)
    project(FAR, 1)
    pass_wo(2)
    arrived(BEHIND2, 1)
    arrived(AHEAD2, 0)
    project(BEHIND2, 2)
    docs_arrived(6, 0, 2)
    docs_arrived(7, 1, 2)
    arrived(FAR2, 0)
    arrived(FAR2, 1)
    project(FAR2, 1)
    pass_wo(3)
    for slot in range(8):
        dh, dy = SLOTS[slot]
        ref = kv.at[PAD + 2 * block_of(dh, dy) + 1 - core]
        remote(ref, ref, kvs_sem.at[slot], kvr_sem.at[slot], twin).wait_recv()

    factor = HD ** (-0.5) * LOG2E

    def attend(dh, dy):
        block = 2 * block_of(dh, dy) + core
        heads = q[dh * YS + dy].reshape(4 * BLK, HD)
        keys = kv[pl.ds(block, WIN), :, :HD].reshape(WIN * BLK, HD)
        values = kv[pl.ds(block, WIN), :, HD:].reshape(WIN * BLK, HD)
        scores = lax.dot_general(
            heads, keys, (((1,), (1,)), ((), ())), preferred_element_type=jnp.float32
        ).reshape(4, BLK, WIN * BLK)
        key_docs = dc[pl.ds(block, WIN)].astype(jnp.float32)
        row_docs = jnp.broadcast_to(key_docs[WIN - 1], (BLK, BLK)).T
        tiles = []
        for index in range(WIN):
            same = row_docs == key_docs[index]
            if index == WIN - 1:
                same = same & (
                    lax.broadcasted_iota(jnp.int32, (BLK, BLK), 1)
                    <= lax.broadcasted_iota(jnp.int32, (BLK, BLK), 0)
                )
            tiles.append(
                jnp.where(same[None], scores[:, :, index * BLK : (index + 1) * BLK], -jnp.inf)
            )
        top = functools.reduce(jnp.maximum, tiles)
        top = jnp.max(top, axis=-1, keepdims=True) * factor
        tiles = [jnp.exp2(tile * factor - top) for tile in tiles]
        total = jnp.sum(functools.reduce(jnp.add, tiles), axis=-1, keepdims=True)
        probs = jnp.concatenate([tile.astype(jnp.bfloat16) for tile in tiles], axis=-1)
        res = jnp.dot(
            probs.reshape(4 * BLK, WIN * BLK), values, preferred_element_type=jnp.float32
        ).reshape(4, BLK, HD)
        return (res / total).astype(jnp.bfloat16)

    def att_copy(dy):
        return remote(att_out.at[dy], att.at[1, dy], ats_sem.at[dy], atr_sem.at[dy], across)

    def attend_other(dy, carry):
        res = attend(1, dy)
        for head in range(4):
            att_out[dy, :, head * HD : (head + 1) * HD] = res[head]
        att_copy(dy).start()
        return carry

    def attend_own(dy, carry):
        res = attend(0, dy)
        for head in range(4):
            att[0, dy, :, head * HD : (head + 1) * HD] = res[head]
        return carry

    lax.fori_loop(0, YS, attend_other, 0)
    pass_wo(4)
    lax.fori_loop(0, YS, attend_own, 0)

    own_wo = wo.at[0, pl.ds(pl.multiple_of((1 - core) * 256, 256), 256), :]
    remote(own_wo, own_wo, wos_sem.at[2 * NW], wor_sem.at[2 * NW], twin).wait_recv()
    for dy in range(YS):
        att_copy(dy).wait_recv()

    def half_copies(k):
        return (
            remote(far.at[k, FIRST, :], half_f.at[k], rs_send.at[0, k], rs_recv.at[0, k], ahead),
            remote(far.at[k, SECOND, :], half_b.at[k], rs_send.at[1, k], rs_recv.at[1, k], behind),
        )

    def full_copies(k):
        return (
            remote(fwd.at[k], got_f.at[k], rs_send.at[2, k], rs_recv.at[2, k], ahead),
            remote(bwd.at[k], got_b.at[k], rs_send.at[3, k], rs_recv.at[3, k], behind),
        )

    def cols(k):
        return pl.ds(pl.multiple_of(k * cw, cw), cw)

    def shift_copy(k):
        return remote(done.at[k], out_ref.at[0, :, cols(k)], sh_send.at[k], sh_recv.at[k], following)

    def step(i, carry):
        for chunk in range(NW):
            @pl.when(i == chunk * (NJ // NW))
            def _():
                ref = wo.at[1, pl.ds(pl.multiple_of((1 - core) * 256, 256), 256), wo_piece(chunk)]
                remote(
                    ref, ref, wos_sem.at[NW + chunk], wor_sem.at[NW + chunk], twin
                ).wait_recv()

        @pl.when(i < NJ)
        def _():
            res = jnp.dot(
                att[0].reshape(YS * BLK, 4 * HD), wo[0, :, cols(i)], preferred_element_type=jnp.float32
            ) + jnp.dot(
                att[1].reshape(YS * BLK, 4 * HD), wo[1, :, cols(i)], preferred_element_type=jnp.float32
            )
            far[i] = res[2 * BLK : 3 * BLK].astype(jnp.bfloat16)
            for copy in half_copies(i):
                copy.start()
            mine[i] = res[:BLK]
            fwd[i] = res[BLK : 2 * BLK].astype(jnp.bfloat16)
            bwd[i] = res[3 * BLK :].astype(jnp.bfloat16)

        @pl.when((i >= 1) & (i <= NJ))
        def _():
            k = i - 1
            first, second = half_copies(k)
            to_f, to_b = full_copies(k)
            first.wait_recv()
            fwd[k, FIRST, :] = (
                fwd[k, FIRST, :].astype(jnp.float32) + half_f[k].astype(jnp.float32)
            ).astype(jnp.bfloat16)
            to_f.start()
            second.wait_recv()
            bwd[k, SECOND, :] = (
                bwd[k, SECOND, :].astype(jnp.float32) + half_b[k].astype(jnp.float32)
            ).astype(jnp.bfloat16)
            to_b.start()

        @pl.when(i >= 2)
        def _():
            k = i - 2
            from_b, from_f = full_copies(k)
            from_b.wait_recv()
            from_f.wait_recv()
            total = mine[k] + got_f[k].astype(jnp.float32) + got_b[k].astype(jnp.float32)
            done[k] = (state[:, cols(k)].astype(jnp.float32) + total).astype(jnp.bfloat16)
            shift_copy(k).start()

        return carry

    lax.fori_loop(0, NJ + 2, step, 0)

    for copy in sent:
        copy.wait_send()
    for dy in range(YS):
        att_copy(dy).wait_send()

    def finish(k, carry):
        for copy in half_copies(k) + full_copies(k):
            copy.wait_send()
        shift_copy(k).wait()
        return carry

    lax.fori_loop(0, NJ, finish, 0)
    remote(docs_ref, odocs_ref, dsend.at[9], drecv.at[9], following).wait_recv()


def local(state, docs, gain, w_query, w_keyval, w_out):
    width = state.shape[2]
    cw = width // NJ
    bf, f32 = jnp.bfloat16, jnp.float32
    dma = pltpu.SemaphoreType.DMA
    anyspace = pl.BlockSpec(memory_space=pl.ANY)
    return tuple(pl.pallas_call(
        body,
        out_shape=(
            jax.ShapeDtypeStruct(state.shape, state.dtype),
            jax.ShapeDtypeStruct(docs.shape, docs.dtype),
        ),
        in_specs=[anyspace] * 6,
        out_specs=(anyspace, anyspace),
        scratch_shapes=[
            pltpu.VMEM((BLK, width), bf),
            pltpu.VMEM((1, width), f32),
            pltpu.VMEM((8, BLK, width), bf),
            pltpu.VMEM((3, width, 2 * HD), bf),
            pltpu.VMEM((2, 4 * HD, width), bf),
            pltpu.VMEM((8, 4, BLK, HD), bf),
            pltpu.VMEM((16 + PAD, BLK, 2 * HD), bf),
            pltpu.VMEM((16 + PAD, 1, BLK), jnp.int32),
            pltpu.VMEM((2, YS, BLK, 4 * HD), bf),
            pltpu.VMEM((YS, BLK, 4 * HD), bf),
            pltpu.VMEM((NJ, BLK, cw), bf),
            pltpu.VMEM((NJ, BLK, cw), bf),
            pltpu.VMEM((NJ, BLK, cw), bf),
            pltpu.VMEM((NJ, BLK, cw), f32),
            pltpu.VMEM((NJ, HALF, cw), bf),
            pltpu.VMEM((NJ, HALF, cw), bf),
            pltpu.VMEM((NJ, BLK, cw), bf),
            pltpu.VMEM((NJ, BLK, cw), bf),
            pltpu.VMEM((NJ, BLK, cw), bf),
            dma((6,)),
            dma((14,)), dma((8, 2)),
            dma((10,)), dma((10,)),
            dma((2,)), dma((2,)),
            dma((8,)), dma((8,)),
            dma((2 * NW + 1,)), dma((2 * NW + 1,)),
            dma((YS,)), dma((YS,)),
            dma((4, NJ)), dma((4, NJ)),
            dma((NJ,)), dma((NJ,)),
        ],
        compiler_params=pltpu.CompilerParams(
            collective_id=0, has_side_effects=True, vmem_limit_bytes=60 << 20
        ),
        name="layer",
    )(state, docs, gain, w_query, w_keyval, w_out))


def solution(mesh):
    in_specs = (
        P("section", "tensor", None),
        P("section", "tensor"),
        P("section", None),
        P("section", None, "tensor"),
        P("section", None, "tensor"),
        P("section", "tensor", None),
    )
    out_specs = (P("section", "tensor", None), P("section", "tensor"))
    return jax.shard_map(local, mesh=mesh, in_specs=in_specs, out_specs=out_specs, check_vma=False)
```

```python
import functools

import jax
import jax.numpy as jnp
from jax import lax
from jax.experimental import pallas as pl
from jax.experimental.pallas import tpu as pltpu
from jax.sharding import PartitionSpec as P

MESH = pl.DeviceIdType.MESH
BLK = 128
HALF = 64
HD = 128
WIN = 5
PAD = WIN - 1
YS = 4
NJ = 10
LAG = 3
NW = 5
SLOTS = ((0, 0), (1, 0), (0, 3), (0, 1), (1, 3), (1, 1), (0, 2), (1, 2))
OWN, ACROSS, BEHIND, AHEAD, BEHIND2, AHEAD2, FAR, FAR2 = range(8)
LOG2E = 1.4426950408889634
FIRST = pl.ds(0, HALF)
SECOND = pl.ds(HALF, HALF)


def body(
    state_ref, docs_ref, gain_ref, wq_ref, wkv_ref, wo_ref,
    out_ref, odocs_ref,
    state, gain, xg, w, wo, q, kv, dc, att,
    far, fwd, bwd, half_f, half_b, got_f, got_b, done,
    load_sem, xs_sem, xr_sem, dsend, drecv, ws_sem, wr_sem, kvs_sem, kvr_sem,
    wos_sem, wor_sem, ats_sem, atr_sem, rs_send, rs_recv, sh_send, sh_recv,
):
    width = state.shape[1]
    cw = width // NJ
    ww = width // NW
    sec = lax.axis_index("section")
    ten = lax.axis_index("tensor")
    nsec = lax.axis_size("section")
    xh, y, core = ten // (2 * YS), (ten // 2) % YS, ten % 2

    def at(dh, dy, dcore=0):
        return (sec, ((xh + dh) % 2) * (2 * YS) + ((y + dy) % YS) * 2 + (core + dcore) % 2)

    def block_of(dh, dy):
        return ((xh + dh) % 2) * YS + (y + dy) % YS

    twin, across, ahead, behind = at(0, 0, 1), at(1, 0), at(0, 1), at(0, 3)
    following = ((sec + 1) % nsec, ten)
    before = ((sec + nsec - 1) % nsec, ten)

    loads = [
        pltpu.make_async_copy(state_ref.at[0], state, load_sem.at[0]),
        pltpu.make_async_copy(gain_ref, gain, load_sem.at[1]),
        pltpu.make_async_copy(docs_ref, dc.at[PAD + 2 * block_of(0, 0) + core], load_sem.at[2]),
        pltpu.make_async_copy(wq_ref.at[0], w.at[core], load_sem.at[3]),
        pltpu.make_async_copy(
            wkv_ref.at[0], w.at[2, :, pl.ds(pl.multiple_of(core * HD, HD), HD)], load_sem.at[4]
        ),
        pltpu.make_async_copy(
            wo_ref.at[0], wo.at[0, pl.ds(pl.multiple_of(core * 256, 256), 256), :], load_sem.at[5]
        ),
    ]
    for copy in loads:
        copy.start()

    barrier = pltpu.get_barrier_semaphore()
    for other in (twin, across, ahead, behind, following, before):
        pl.semaphore_signal(barrier, inc=1, device_id=other, device_id_type=MESH)

    for index in range(PAD):
        kv[index] = jnp.zeros((BLK, 2 * HD), jnp.bfloat16)
        dc[index] = jnp.full((1, BLK), -1, jnp.int32)

    def remote(src, dst, send, recv, target):
        return pltpu.make_async_remote_copy(
            src_ref=src, dst_ref=dst, send_sem=send, recv_sem=recv, device_id=target, device_id_type=MESH
        )

    sent = []

    def go(copy):
        copy.start()
        sent.append(copy)
        return copy

    def piece(number, src, dst, part, target):
        rows = FIRST if part == 0 else SECOND
        return remote(
            xg.at[src, rows, :], xg.at[dst, rows, :], xs_sem.at[number], xr_sem.at[dst, part], target
        )

    def arrived(slot, part):
        rows = FIRST if part == 0 else SECOND
        remote(
            xg.at[slot, rows, :], xg.at[slot, rows, :], xs_sem.at[0], xr_sem.at[slot, part], twin
        ).wait_recv()

    def doc_pair(dh, dy):
        return dc.at[pl.ds(PAD + 2 * block_of(dh, dy), 2)]

    def send_docs(number, dh, dy, recv, target):
        ref = doc_pair(dh, dy)
        return remote(ref, ref, dsend.at[number], drecv.at[recv], target)

    def docs_arrived(recv, dh, dy):
        ref = doc_pair(dh, dy)
        remote(ref, ref, dsend.at[0], drecv.at[recv], twin).wait_recv()

    loads[0].wait()
    loads[1].wait()

    def norm(rows):
        wide = state[rows, :].astype(jnp.float32)
        factor = lax.rsqrt(jnp.mean(wide * wide, axis=-1, keepdims=True) + 1e-05)
        xg[OWN, rows, :] = (wide * factor * gain[...]).astype(jnp.bfloat16)

    norm(FIRST)
    pl.semaphore_wait(barrier, 6)
    go(piece(0, OWN, BEHIND, 0, ahead))
    across_first = piece(1, OWN, ACROSS, 0, across)
    across_first.start()
    norm(SECOND)
    go(piece(2, OWN, AHEAD, 1, behind))
    go(piece(3, OWN, BEHIND, 1, ahead))
    go(piece(4, OWN, AHEAD, 0, behind))

    loads[2].wait()
    own_docs = dc.at[PAD + 2 * block_of(0, 0) + core]
    go(remote(own_docs, own_docs, dsend.at[0], drecv.at[0], twin))
    go(remote(docs_ref, odocs_ref, dsend.at[9], drecv.at[9], following))
    go(remote(wq_ref.at[0], w.at[core], ws_sem.at[0], wr_sem.at[0], twin))
    kv_cols = w.at[2, :, pl.ds(pl.multiple_of(core * HD, HD), HD)]
    go(remote(wkv_ref.at[0], kv_cols, ws_sem.at[1], wr_sem.at[1], twin))
    twin_docs = dc.at[PAD + 2 * block_of(0, 0) + 1 - core]
    remote(twin_docs, twin_docs, dsend.at[0], drecv.at[0], twin).wait_recv()
    go(send_docs(1, 0, 0, 1, across))
    go(send_docs(2, 0, 0, 2, ahead))
    go(send_docs(3, 0, 0, 3, behind))

    def project(slot, count):
        rows = xg[pl.ds(slot, count)].reshape(count * BLK, width)
        for index in (2, 0, 1):
            res = jnp.dot(rows, w[index], preferred_element_type=jnp.float32).astype(jnp.bfloat16)
            for one in range(count):
                dh, dy = SLOTS[slot + one]
                part = res[one * BLK : (one + 1) * BLK]
                if index < 2:
                    q[dh * YS + dy, 2 * index] = part[:, :HD]
                    q[dh * YS + dy, 2 * index + 1] = part[:, HD:]
                else:
                    ref = kv.at[PAD + 2 * block_of(dh, dy) + core]
                    ref[...] = part
                    go(remote(ref, ref, kvs_sem.at[slot + one], kvr_sem.at[slot + one], twin))

    def wo_piece(chunk):
        return pl.ds(chunk * ww, ww)

    def wo_across(chunk):
        dst = wo.at[1, pl.ds(pl.multiple_of(core * 256, 256), 256), wo_piece(chunk)]
        return remote(wo_ref.at[0, :, wo_piece(chunk)], dst, wos_sem.at[chunk], wor_sem.at[chunk], across)

    def wo_relay(chunk):
        ref = wo.at[1, pl.ds(pl.multiple_of(core * 256, 256), 256), wo_piece(chunk)]
        return remote(ref, ref, wos_sem.at[NW + chunk], wor_sem.at[NW + chunk], twin)

    def pass_wo(chunk):
        wo_across(chunk).wait_recv()
        go(wo_relay(chunk))

    across_first.wait_send()
    across_last = piece(5, OWN, ACROSS, 1, across)
    across_last.start()
    arrived(ACROSS, 0)
    go(piece(8, ACROSS, BEHIND2, 0, ahead))
    go(piece(10, ACROSS, AHEAD2, 0, behind))
    arrived(BEHIND, 0)
    go(piece(6, BEHIND, FAR, 0, ahead))
    arrived(AHEAD, 1)
    go(piece(7, AHEAD, FAR, 1, behind))
    arrived(ACROSS, 1)
    go(piece(9, ACROSS, AHEAD2, 1, behind))
    go(piece(11, ACROSS, BEHIND2, 1, ahead))
    across_last.wait_send()
    for chunk in range(3):
        go(wo_across(chunk))
    docs_arrived(1, 1, 0)
    go(send_docs(4, 1, 0, 4, ahead))
    go(send_docs(5, 1, 0, 5, behind))
    docs_arrived(2, 0, 3)
    go(send_docs(6, 0, 3, 6, ahead))
    docs_arrived(3, 0, 1)
    go(remote(
        wo_ref.at[0], wo.at[0, pl.ds(pl.multiple_of(core * 256, 256), 256), :],
        wos_sem.at[2 * NW], wor_sem.at[2 * NW], twin,
    ))

    for copy in loads[3:]:
        copy.wait()
    remote(w.at[1 - core], w.at[1 - core], ws_sem.at[0], wr_sem.at[0], twin).wait_recv()
    kv_cols2 = w.at[2, :, pl.ds(pl.multiple_of((1 - core) * HD, HD), HD)]
    remote(kv_cols2, kv_cols2, ws_sem.at[1], wr_sem.at[1], twin).wait_recv()
    project(OWN, 2)
    docs_arrived(4, 1, 3)
    go(send_docs(7, 1, 3, 7, ahead))
    docs_arrived(5, 1, 1)
    arrived(BEHIND, 1)
    arrived(AHEAD, 0)
    project(BEHIND, 2)
    go(wo_across(3))
    arrived(BEHIND2, 0)
    go(piece(12, BEHIND2, FAR2, 0, ahead))
    arrived(AHEAD2, 1)
    go(piece(13, AHEAD2, FAR2, 1, behind))
    arrived(FAR, 0)
    arrived(FAR, 1)
    project(FAR, 1)
    go(wo_across(4))
    pass_wo(0)
    arrived(BEHIND2, 1)
    arrived(AHEAD2, 0)
    project(BEHIND2, 2)
    pass_wo(1)
    docs_arrived(6, 0, 2)
    docs_arrived(7, 1, 2)
    arrived(FAR2, 0)
    arrived(FAR2, 1)
    project(FAR2, 1)
    pass_wo(2)
    pass_wo(3)
    for slot in range(8):
        dh, dy = SLOTS[slot]
        ref = kv.at[PAD + 2 * block_of(dh, dy) + 1 - core]
        remote(ref, ref, kvs_sem.at[slot], kvr_sem.at[slot], twin).wait_recv()

    factor = HD ** (-0.5) * LOG2E

    def attend(dh, dy):
        block = 2 * block_of(dh, dy) + core
        heads = q[dh * YS + dy].reshape(4 * BLK, HD)
        keys = kv[pl.ds(block, WIN), :, :HD].reshape(WIN * BLK, HD)
        values = kv[pl.ds(block, WIN), :, HD:].reshape(WIN * BLK, HD)
        scores = lax.dot_general(
            heads, keys, (((1,), (1,)), ((), ())), preferred_element_type=jnp.float32
        ).reshape(4, BLK, WIN * BLK)
        key_docs = dc[pl.ds(block, WIN)].astype(jnp.float32)
        row_docs = jnp.broadcast_to(key_docs[WIN - 1], (BLK, BLK)).T
        tiles = []
        for index in range(WIN):
            same = row_docs == key_docs[index]
            if index == WIN - 1:
                same = same & (
                    lax.broadcasted_iota(jnp.int32, (BLK, BLK), 1)
                    <= lax.broadcasted_iota(jnp.int32, (BLK, BLK), 0)
                )
            tiles.append(
                jnp.where(same[None], scores[:, :, index * BLK : (index + 1) * BLK], -jnp.inf)
            )
        top = functools.reduce(jnp.maximum, tiles)
        top = jnp.max(top, axis=-1, keepdims=True) * factor
        tiles = [jnp.exp2(tile * factor - top) for tile in tiles]
        total = jnp.sum(functools.reduce(jnp.add, tiles), axis=-1, keepdims=True)
        probs = jnp.concatenate([tile.astype(jnp.bfloat16) for tile in tiles], axis=-1)
        res = jnp.dot(
            probs.reshape(4 * BLK, WIN * BLK), values, preferred_element_type=jnp.float32
        ).reshape(4, BLK, HD)
        return (res / total).astype(jnp.bfloat16)

    def att_copy(place):
        return remote(att.at[2, place], att.at[1, place], ats_sem.at[place], atr_sem.at[place], across)

    def attend_all(order):
        def one(i, carry):
            code = jnp.int32(order[-1])
            for index in range(len(order) - 1):
                code = jnp.where(i == index, order[index], code)
            dh, place = code // YS, code % YS
            dy = jnp.where(place < 2, 2 - place, 9 - 3 * place)
            res = attend(dh, dy)
            for head in range(4):
                att[2 * dh, place, :, head * HD : (head + 1) * HD] = res[head]

            @pl.when(dh == 1)
            def _():
                att_copy(place).start()

            return carry

        lax.fori_loop(0, len(order), one, 0)

    attend_all((4, 0, 1, 5, 6))
    pass_wo(4)
    own_wo = wo.at[0, pl.ds(pl.multiple_of((1 - core) * 256, 256), 256), :]
    remote(own_wo, own_wo, wos_sem.at[2 * NW], wor_sem.at[2 * NW], twin).wait_recv()
    att_copy(0).wait_recv()

    def half_copies(k):
        return (
            remote(far.at[k, FIRST, :], half_f.at[k], rs_send.at[0, k], rs_recv.at[0, k], ahead),
            remote(far.at[k, SECOND, :], half_b.at[k], rs_send.at[1, k], rs_recv.at[1, k], behind),
        )

    def full_copies(k):
        return (
            remote(fwd.at[k], got_f.at[k], rs_send.at[2, k], rs_recv.at[2, k], ahead),
            remote(bwd.at[k], got_b.at[k], rs_send.at[3, k], rs_recv.at[3, k], behind),
        )

    def cols(k):
        return pl.ds(pl.multiple_of(k * cw, cw), cw)

    def shift_copy(k):
        return remote(done.at[k], out_ref.at[0, :, cols(k)], sh_send.at[k], sh_recv.at[k], following)

    def product(first, count, k):
        return sum(
            jnp.dot(
                att[group, pl.ds(first, count)].reshape(count * BLK, 4 * HD),
                wo[group, :, cols(k)],
                preferred_element_type=jnp.float32,
            )
            for group in range(2)
        )

    def far_step(i, carry):
        for chunk in range(NW):
            @pl.when(i == chunk * (NJ // NW))
            def _():
                ref = wo.at[1, pl.ds(pl.multiple_of((1 - core) * 256, 256), 256), wo_piece(chunk)]
                remote(
                    ref, ref, wos_sem.at[NW + chunk], wor_sem.at[NW + chunk], twin
                ).wait_recv()

        far[i] = product(0, 1, i).astype(jnp.bfloat16)
        for copy in half_copies(i):
            copy.start()
        return carry

    lax.fori_loop(0, NJ, far_step, 0)
    attend_all((2, 7, 3))
    att_copy(1).wait_recv()
    att_copy(2).wait_recv()

    def step(i, carry):
        @pl.when(i < NJ)
        def _():
            res = product(1, 2, i)
            first, second = half_copies(i)
            to_f, to_b = full_copies(i)
            first.wait_recv()
            fwd[i, SECOND, :] = res[HALF:BLK].astype(jnp.bfloat16)
            fwd[i, FIRST, :] = (res[:HALF] + half_f[i].astype(jnp.float32)).astype(jnp.bfloat16)
            to_f.start()
            second.wait_recv()
            bwd[i, FIRST, :] = res[BLK : BLK + HALF].astype(jnp.bfloat16)
            bwd[i, SECOND, :] = (res[BLK + HALF :] + half_b[i].astype(jnp.float32)).astype(jnp.bfloat16)
            to_b.start()

        @pl.when(i == LAG)
        def _():
            att_copy(3).wait_recv()

        @pl.when(i >= LAG)
        def _():
            k = i - LAG
            total = state[:, cols(k)].astype(jnp.float32) + product(3, 1, k)
            from_b, from_f = full_copies(k)
            from_b.wait_recv()
            from_f.wait_recv()
            total = total + got_f[k].astype(jnp.float32) + got_b[k].astype(jnp.float32)
            done[k] = total.astype(jnp.bfloat16)
            shift_copy(k).start()

        return carry

    lax.fori_loop(0, NJ + LAG, step, 0)

    for copy in sent:
        copy.wait_send()
    for place in range(YS):
        att_copy(place).wait_send()

    def finish(k, carry):
        for copy in half_copies(k) + full_copies(k):
            copy.wait_send()
        shift_copy(k).wait()
        return carry

    lax.fori_loop(0, NJ, finish, 0)
    remote(docs_ref, odocs_ref, dsend.at[9], drecv.at[9], following).wait_recv()


def local(state, docs, gain, w_query, w_keyval, w_out):
    width = state.shape[2]
    cw = width // NJ
    bf, f32 = jnp.bfloat16, jnp.float32
    dma = pltpu.SemaphoreType.DMA
    anyspace = pl.BlockSpec(memory_space=pl.ANY)
    return tuple(pl.pallas_call(
        body,
        out_shape=(
            jax.ShapeDtypeStruct(state.shape, state.dtype),
            jax.ShapeDtypeStruct(docs.shape, docs.dtype),
        ),
        in_specs=[anyspace] * 6,
        out_specs=(anyspace, anyspace),
        scratch_shapes=[
            pltpu.VMEM((BLK, width), bf),
            pltpu.VMEM((1, width), f32),
            pltpu.VMEM((8, BLK, width), bf),
            pltpu.VMEM((3, width, 2 * HD), bf),
            pltpu.VMEM((2, 4 * HD, width), bf),
            pltpu.VMEM((8, 4, BLK, HD), bf),
            pltpu.VMEM((16 + PAD, BLK, 2 * HD), bf),
            pltpu.VMEM((16 + PAD, 1, BLK), jnp.int32),
            pltpu.VMEM((3, YS, BLK, 4 * HD), bf),
            pltpu.VMEM((NJ, BLK, cw), bf),
            pltpu.VMEM((NJ, BLK, cw), bf),
            pltpu.VMEM((NJ, BLK, cw), bf),
            pltpu.VMEM((NJ, HALF, cw), bf),
            pltpu.VMEM((NJ, HALF, cw), bf),
            pltpu.VMEM((NJ, BLK, cw), bf),
            pltpu.VMEM((NJ, BLK, cw), bf),
            pltpu.VMEM((NJ, BLK, cw), bf),
            dma((6,)),
            dma((14,)), dma((8, 2)),
            dma((10,)), dma((10,)),
            dma((2,)), dma((2,)),
            dma((8,)), dma((8,)),
            dma((2 * NW + 1,)), dma((2 * NW + 1,)),
            dma((YS,)), dma((YS,)),
            dma((4, NJ)), dma((4, NJ)),
            dma((NJ,)), dma((NJ,)),
        ],
        compiler_params=pltpu.CompilerParams(
            collective_id=0, has_side_effects=True, vmem_limit_bytes=60 << 20
        ),
        name="layer",
    )(state, docs, gain, w_query, w_keyval, w_out))


def solution(mesh):
    in_specs = (
        P("section", "tensor", None),
        P("section", "tensor"),
        P("section", None),
        P("section", None, "tensor"),
        P("section", None, "tensor"),
        P("section", "tensor", None),
    )
    out_specs = (P("section", "tensor", None), P("section", "tensor"))
    return jax.shard_map(local, mesh=mesh, in_specs=in_specs, out_specs=out_specs, check_vma=False)
```

```python
import functools

import jax
import jax.numpy as jnp
from jax import lax
from jax.experimental import pallas as pl
from jax.experimental.pallas import tpu as pltpu
from jax.sharding import PartitionSpec as P

MESH = pl.DeviceIdType.MESH
BLK = 128
HALF = 64
HD = 128
WIN = 5
PAD = WIN - 1
YS = 4
NJ = 20
LAG = 7
NW = 5
SLOTS = ((0, 0), (1, 0), (0, 3), (0, 1), (1, 3), (1, 1), (0, 2), (1, 2))
OWN, ACROSS, BEHIND, AHEAD, BEHIND2, AHEAD2, FAR, FAR2 = range(8)
LOG2E = 1.4426950408889634
FIRST = pl.ds(0, HALF)
SECOND = pl.ds(HALF, HALF)


def body(
    state_ref, docs_ref, gain_ref, wq_ref, wkv_ref, wo_ref,
    out_ref, odocs_ref,
    state, gain, xg, w, wo, q, kv, dc, att,
    far, fwd, bwd, half_f, half_b, got_f, got_b, done,
    load_sem, xs_sem, xr_sem, dsend, drecv, ws_sem, wr_sem, kvs_sem, kvr_sem,
    wos_sem, wor_sem, ats_sem, atr_sem, rs_send, rs_recv, sh_send, sh_recv,
):
    width = state.shape[1]
    cw = width // NJ
    ww = width // NW
    sec = lax.axis_index("section")
    ten = lax.axis_index("tensor")
    nsec = lax.axis_size("section")
    xh, y, core = ten // (2 * YS), (ten // 2) % YS, ten % 2

    def at(dh, dy, dcore=0):
        return (sec, ((xh + dh) % 2) * (2 * YS) + ((y + dy) % YS) * 2 + (core + dcore) % 2)

    def block_of(dh, dy):
        return ((xh + dh) % 2) * YS + (y + dy) % YS

    twin, across, ahead, behind = at(0, 0, 1), at(1, 0), at(0, 1), at(0, 3)
    following = ((sec + 1) % nsec, ten)
    before = ((sec + nsec - 1) % nsec, ten)

    loads = [
        pltpu.make_async_copy(state_ref.at[0], state, load_sem.at[0]),
        pltpu.make_async_copy(gain_ref, gain, load_sem.at[1]),
        pltpu.make_async_copy(docs_ref, dc.at[PAD + 2 * block_of(0, 0) + core], load_sem.at[2]),
        pltpu.make_async_copy(wq_ref.at[0], w.at[core], load_sem.at[3]),
        pltpu.make_async_copy(
            wkv_ref.at[0], w.at[2, :, pl.ds(pl.multiple_of(core * HD, HD), HD)], load_sem.at[4]
        ),
        pltpu.make_async_copy(
            wo_ref.at[0], wo.at[0, pl.ds(pl.multiple_of(core * 256, 256), 256), :], load_sem.at[5]
        ),
    ]
    for copy in loads:
        copy.start()

    barrier = pltpu.get_barrier_semaphore()
    for other in (twin, across, ahead, behind, following, before):
        pl.semaphore_signal(barrier, inc=1, device_id=other, device_id_type=MESH)

    for index in range(PAD):
        kv[index] = jnp.zeros((BLK, 2 * HD), jnp.bfloat16)
        dc[index] = jnp.full((1, BLK), -1, jnp.int32)

    def remote(src, dst, send, recv, target):
        return pltpu.make_async_remote_copy(
            src_ref=src, dst_ref=dst, send_sem=send, recv_sem=recv, device_id=target, device_id_type=MESH
        )

    sent = []

    def go(copy):
        copy.start()
        sent.append(copy)
        return copy

    def piece(number, src, dst, part, target):
        rows = FIRST if part == 0 else SECOND
        return remote(
            xg.at[src, rows, :], xg.at[dst, rows, :], xs_sem.at[number], xr_sem.at[dst, part], target
        )

    def arrived(slot, part):
        rows = FIRST if part == 0 else SECOND
        remote(
            xg.at[slot, rows, :], xg.at[slot, rows, :], xs_sem.at[0], xr_sem.at[slot, part], twin
        ).wait_recv()

    def doc_pair(dh, dy):
        return dc.at[pl.ds(PAD + 2 * block_of(dh, dy), 2)]

    def send_docs(number, dh, dy, recv, target):
        ref = doc_pair(dh, dy)
        return remote(ref, ref, dsend.at[number], drecv.at[recv], target)

    def docs_arrived(recv, dh, dy):
        ref = doc_pair(dh, dy)
        remote(ref, ref, dsend.at[0], drecv.at[recv], twin).wait_recv()

    loads[0].wait()
    loads[1].wait()

    def norm(rows):
        wide = state[rows, :].astype(jnp.float32)
        factor = lax.rsqrt(jnp.mean(wide * wide, axis=-1, keepdims=True) + 1e-05)
        xg[OWN, rows, :] = (wide * factor * gain[...]).astype(jnp.bfloat16)

    norm(FIRST)
    pl.semaphore_wait(barrier, 6)
    go(piece(0, OWN, BEHIND, 0, ahead))
    across_first = piece(1, OWN, ACROSS, 0, across)
    across_first.start()
    norm(SECOND)
    go(piece(2, OWN, AHEAD, 1, behind))
    go(piece(3, OWN, BEHIND, 1, ahead))
    go(piece(4, OWN, AHEAD, 0, behind))

    loads[2].wait()
    own_docs = dc.at[PAD + 2 * block_of(0, 0) + core]
    go(remote(own_docs, own_docs, dsend.at[0], drecv.at[0], twin))
    go(remote(docs_ref, odocs_ref, dsend.at[9], drecv.at[9], following))
    go(remote(wq_ref.at[0], w.at[core], ws_sem.at[0], wr_sem.at[0], twin))
    kv_cols = w.at[2, :, pl.ds(pl.multiple_of(core * HD, HD), HD)]
    go(remote(wkv_ref.at[0], kv_cols, ws_sem.at[1], wr_sem.at[1], twin))
    twin_docs = dc.at[PAD + 2 * block_of(0, 0) + 1 - core]
    remote(twin_docs, twin_docs, dsend.at[0], drecv.at[0], twin).wait_recv()
    go(send_docs(1, 0, 0, 1, across))
    go(send_docs(2, 0, 0, 2, ahead))
    go(send_docs(3, 0, 0, 3, behind))

    def project(slot, count):
        rows = xg[pl.ds(slot, count)].reshape(count * BLK, width)
        for index in (2, 0, 1):
            res = jnp.dot(rows, w[index], preferred_element_type=jnp.float32).astype(jnp.bfloat16)
            for one in range(count):
                dh, dy = SLOTS[slot + one]
                part = res[one * BLK : (one + 1) * BLK]
                if index < 2:
                    q[dh * YS + dy, 2 * index] = part[:, :HD]
                    q[dh * YS + dy, 2 * index + 1] = part[:, HD:]
                else:
                    ref = kv.at[PAD + 2 * block_of(dh, dy) + core]
                    ref[...] = part
                    go(remote(ref, ref, kvs_sem.at[slot + one], kvr_sem.at[slot + one], twin))

    def wo_piece(chunk):
        return pl.ds(chunk * ww, ww)

    def wo_across(chunk):
        dst = wo.at[1, pl.ds(pl.multiple_of(core * 256, 256), 256), wo_piece(chunk)]
        return remote(wo_ref.at[0, :, wo_piece(chunk)], dst, wos_sem.at[chunk], wor_sem.at[chunk], across)

    def wo_relay(chunk):
        ref = wo.at[1, pl.ds(pl.multiple_of(core * 256, 256), 256), wo_piece(chunk)]
        return remote(ref, ref, wos_sem.at[NW + chunk], wor_sem.at[NW + chunk], twin)

    def pass_wo(chunk):
        wo_across(chunk).wait_recv()
        go(wo_relay(chunk))

    across_first.wait_send()
    across_last = piece(5, OWN, ACROSS, 1, across)
    across_last.start()
    arrived(ACROSS, 0)
    go(piece(8, ACROSS, BEHIND2, 0, ahead))
    go(piece(10, ACROSS, AHEAD2, 0, behind))
    arrived(ACROSS, 1)
    go(piece(9, ACROSS, AHEAD2, 1, behind))
    last_ahead = piece(11, ACROSS, BEHIND2, 1, ahead)
    last_ahead.start()
    across_last.wait_send()
    for chunk in range(3):
        go(wo_across(chunk))
    docs_arrived(1, 1, 0)
    go(send_docs(4, 1, 0, 4, ahead))
    go(send_docs(5, 1, 0, 5, behind))
    docs_arrived(2, 0, 3)
    go(send_docs(6, 0, 3, 6, ahead))
    docs_arrived(3, 0, 1)
    go(remote(
        wo_ref.at[0], wo.at[0, pl.ds(pl.multiple_of(core * 256, 256), 256), :],
        wos_sem.at[2 * NW], wor_sem.at[2 * NW], twin,
    ))

    for copy in loads[3:]:
        copy.wait()
    remote(w.at[1 - core], w.at[1 - core], ws_sem.at[0], wr_sem.at[0], twin).wait_recv()
    kv_cols2 = w.at[2, :, pl.ds(pl.multiple_of((1 - core) * HD, HD), HD)]
    remote(kv_cols2, kv_cols2, ws_sem.at[1], wr_sem.at[1], twin).wait_recv()
    project(OWN, 2)
    docs_arrived(4, 1, 3)
    go(send_docs(7, 1, 3, 7, ahead))
    docs_arrived(5, 1, 1)
    def twin_keys(slots):
        for slot in slots:
            dh, dy = SLOTS[slot]
            ref = kv.at[PAD + 2 * block_of(dh, dy) + 1 - core]
            remote(ref, ref, kvs_sem.at[slot], kvr_sem.at[slot], twin).wait_recv()

    factor = HD ** (-0.5) * LOG2E

    def attend(dh, dy):
        block = 2 * block_of(dh, dy) + core
        heads = q[dh * YS + dy].reshape(4 * BLK, HD)
        keys = kv[pl.ds(block, WIN), :, :HD].reshape(WIN * BLK, HD)
        values = kv[pl.ds(block, WIN), :, HD:].reshape(WIN * BLK, HD)
        scores = lax.dot_general(
            heads, keys, (((1,), (1,)), ((), ())), preferred_element_type=jnp.float32
        ).reshape(4, BLK, WIN * BLK)
        key_docs = dc[pl.ds(block, WIN)].astype(jnp.float32)
        row_docs = jnp.broadcast_to(key_docs[WIN - 1], (BLK, BLK)).T
        tiles = []
        for index in range(WIN):
            same = row_docs == key_docs[index]
            if index == WIN - 1:
                same = same & (
                    lax.broadcasted_iota(jnp.int32, (BLK, BLK), 1)
                    <= lax.broadcasted_iota(jnp.int32, (BLK, BLK), 0)
                )
            tiles.append(
                jnp.where(same[None], scores[:, :, index * BLK : (index + 1) * BLK], -jnp.inf)
            )
        top = functools.reduce(jnp.maximum, tiles)
        top = jnp.max(top, axis=-1, keepdims=True) * factor
        tiles = [jnp.exp2(tile * factor - top) for tile in tiles]
        total = jnp.sum(functools.reduce(jnp.add, tiles), axis=-1, keepdims=True)
        probs = jnp.concatenate([tile.astype(jnp.bfloat16) for tile in tiles], axis=-1)
        res = jnp.dot(
            probs.reshape(4 * BLK, WIN * BLK), values, preferred_element_type=jnp.float32
        ).reshape(4, BLK, HD)
        return (res / total).astype(jnp.bfloat16)

    def att_copy(place):
        return remote(att.at[2, place], att.at[1, place], ats_sem.at[place], atr_sem.at[place], across)

    def attend_all(order):
        def one(i, carry):
            code = jnp.int32(order[-1])
            for index in range(len(order) - 1):
                code = jnp.where(i == index, order[index], code)
            dh, place = code // YS, code % YS
            dy = jnp.where(place < 2, 2 - place, 9 - 3 * place)
            res = attend(dh, dy)
            for head in range(4):
                att[2 * dh, place, :, head * HD : (head + 1) * HD] = res[head]

            @pl.when(dh == 1)
            def _():
                att_copy(place).start()

            return carry

        lax.fori_loop(0, len(order), one, 0)

    for slot in (BEHIND, AHEAD):
        for part in range(2):
            arrived(slot, part)
    project(BEHIND, 2)
    go(wo_across(3))
    arrived(BEHIND2, 0)
    go(piece(12, BEHIND2, FAR2, 0, ahead))
    arrived(AHEAD2, 1)
    go(piece(13, AHEAD2, FAR2, 1, behind))
    last_ahead.wait_send()
    go(piece(6, BEHIND, FAR, 0, ahead))
    go(piece(7, AHEAD, FAR, 1, behind))
    go(wo_across(4))
    pass_wo(0)
    arrived(BEHIND2, 1)
    arrived(AHEAD2, 0)
    project(BEHIND2, 2)
    pass_wo(1)
    docs_arrived(6, 0, 2)
    docs_arrived(7, 1, 2)
    arrived(FAR2, 0)
    arrived(FAR2, 1)
    project(FAR2, 1)
    twin_keys((OWN, ACROSS, BEHIND, AHEAD, BEHIND2, AHEAD2, FAR2))
    attend_all((4, 5, 1))
    pass_wo(2)
    pass_wo(3)
    arrived(FAR, 0)
    arrived(FAR, 1)
    project(FAR, 1)
    twin_keys((FAR,))
    attend_all((0, 6))
    pass_wo(4)
    own_wo = wo.at[0, pl.ds(pl.multiple_of((1 - core) * 256, 256), 256), :]
    remote(own_wo, own_wo, wos_sem.at[2 * NW], wor_sem.at[2 * NW], twin).wait_recv()
    att_copy(0).wait_recv()

    def half_copies(k):
        return (
            remote(far.at[k, FIRST, :], half_f.at[k], rs_send.at[0, k], rs_recv.at[0, k], ahead),
            remote(far.at[k, SECOND, :], half_b.at[k], rs_send.at[1, k], rs_recv.at[1, k], behind),
        )

    def full_copies(k):
        return (
            remote(fwd.at[k], got_f.at[k], rs_send.at[2, k], rs_recv.at[2, k], ahead),
            remote(bwd.at[k], got_b.at[k], rs_send.at[3, k], rs_recv.at[3, k], behind),
        )

    def cols(k):
        return pl.ds(pl.multiple_of(k * cw, cw), cw)

    def shift_copy(k):
        return remote(done.at[k], out_ref.at[0, :, cols(k)], sh_send.at[k], sh_recv.at[k], following)

    def product(first, count, k):
        return sum(
            jnp.dot(
                att[group, pl.ds(first, count)].reshape(count * BLK, 4 * HD),
                wo[group, :, cols(k)],
                preferred_element_type=jnp.float32,
            )
            for group in range(2)
        )

    def far_step(i, carry):
        for chunk in range(NW):
            @pl.when(i == chunk * (NJ // NW))
            def _():
                ref = wo.at[1, pl.ds(pl.multiple_of((1 - core) * 256, 256), 256), wo_piece(chunk)]
                remote(
                    ref, ref, wos_sem.at[NW + chunk], wor_sem.at[NW + chunk], twin
                ).wait_recv()

        far[i] = product(0, 1, i).astype(jnp.bfloat16)
        for copy in half_copies(i):
            copy.start()
        return carry

    lax.fori_loop(0, NJ, far_step, 0)
    attend_all((7, 2, 3))
    att_copy(1).wait_recv()
    att_copy(2).wait_recv()

    def step(i, carry):
        @pl.when(i < NJ)
        def _():
            res = product(1, 2, i)
            first, second = half_copies(i)
            to_f, to_b = full_copies(i)
            first.wait_recv()
            fwd[i, SECOND, :] = res[HALF:BLK].astype(jnp.bfloat16)
            fwd[i, FIRST, :] = (res[:HALF] + half_f[i].astype(jnp.float32)).astype(jnp.bfloat16)
            to_f.start()
            second.wait_recv()
            bwd[i, FIRST, :] = res[BLK : BLK + HALF].astype(jnp.bfloat16)
            bwd[i, SECOND, :] = (res[BLK + HALF :] + half_b[i].astype(jnp.float32)).astype(jnp.bfloat16)
            to_b.start()

        @pl.when(i == LAG)
        def _():
            att_copy(3).wait_recv()

        @pl.when(i >= LAG)
        def _():
            k = i - LAG
            total = state[:, cols(k)].astype(jnp.float32) + product(3, 1, k)
            from_b, from_f = full_copies(k)
            from_b.wait_recv()
            from_f.wait_recv()
            total = total + got_f[k].astype(jnp.float32) + got_b[k].astype(jnp.float32)
            done[k] = total.astype(jnp.bfloat16)
            shift_copy(k).start()

        return carry

    lax.fori_loop(0, NJ + LAG, step, 0)

    for copy in sent:
        copy.wait_send()
    for place in range(YS):
        att_copy(place).wait_send()

    def finish(k, carry):
        for copy in half_copies(k) + full_copies(k):
            copy.wait_send()
        shift_copy(k).wait()
        return carry

    lax.fori_loop(0, NJ, finish, 0)
    remote(docs_ref, odocs_ref, dsend.at[9], drecv.at[9], following).wait_recv()


def local(state, docs, gain, w_query, w_keyval, w_out):
    width = state.shape[2]
    cw = width // NJ
    bf, f32 = jnp.bfloat16, jnp.float32
    dma = pltpu.SemaphoreType.DMA
    anyspace = pl.BlockSpec(memory_space=pl.ANY)
    return tuple(pl.pallas_call(
        body,
        out_shape=(
            jax.ShapeDtypeStruct(state.shape, state.dtype),
            jax.ShapeDtypeStruct(docs.shape, docs.dtype),
        ),
        in_specs=[anyspace] * 6,
        out_specs=(anyspace, anyspace),
        scratch_shapes=[
            pltpu.VMEM((BLK, width), bf),
            pltpu.VMEM((1, width), f32),
            pltpu.VMEM((8, BLK, width), bf),
            pltpu.VMEM((3, width, 2 * HD), bf),
            pltpu.VMEM((2, 4 * HD, width), bf),
            pltpu.VMEM((8, 4, BLK, HD), bf),
            pltpu.VMEM((16 + PAD, BLK, 2 * HD), bf),
            pltpu.VMEM((16 + PAD, 1, BLK), jnp.int32),
            pltpu.VMEM((3, YS, BLK, 4 * HD), bf),
            pltpu.VMEM((NJ, BLK, cw), bf),
            pltpu.VMEM((NJ, BLK, cw), bf),
            pltpu.VMEM((NJ, BLK, cw), bf),
            pltpu.VMEM((NJ, HALF, cw), bf),
            pltpu.VMEM((NJ, HALF, cw), bf),
            pltpu.VMEM((NJ, BLK, cw), bf),
            pltpu.VMEM((NJ, BLK, cw), bf),
            pltpu.VMEM((NJ, BLK, cw), bf),
            dma((6,)),
            dma((14,)), dma((8, 2)),
            dma((10,)), dma((10,)),
            dma((2,)), dma((2,)),
            dma((8,)), dma((8,)),
            dma((2 * NW + 1,)), dma((2 * NW + 1,)),
            dma((YS,)), dma((YS,)),
            dma((4, NJ)), dma((4, NJ)),
            dma((NJ,)), dma((NJ,)),
        ],
        compiler_params=pltpu.CompilerParams(
            collective_id=0, has_side_effects=True, vmem_limit_bytes=60 << 20
        ),
        name="layer",
    )(state, docs, gain, w_query, w_keyval, w_out))


def solution(mesh):
    in_specs = (
        P("section", "tensor", None),
        P("section", "tensor"),
        P("section", None),
        P("section", None, "tensor"),
        P("section", None, "tensor"),
        P("section", "tensor", None),
    )
    out_specs = (P("section", "tensor", None), P("section", "tensor"))
    return jax.shard_map(local, mesh=mesh, in_specs=in_specs, out_specs=out_specs, check_vma=False)
```

```python
import functools

import jax
import jax.numpy as jnp
from jax import lax
from jax.experimental import pallas as pl
from jax.experimental.pallas import tpu as pltpu
from jax.sharding import PartitionSpec as P

MESH = pl.DeviceIdType.MESH
BLK = 128
HALF = 64
HD = 128
WIN = 5
PAD = WIN - 1
YS = 4
NJ = 20
LAG = 7
NW = 5
SLOTS = ((0, 0), (1, 0), (0, 3), (0, 1), (1, 3), (1, 1), (0, 2), (1, 2))
OWN, ACROSS, BEHIND, AHEAD, BEHIND2, AHEAD2, FAR, FAR2 = range(8)
LOG2E = 1.4426950408889634
FIRST = pl.ds(0, HALF)
SECOND = pl.ds(HALF, HALF)


def body(
    state_ref, docs_ref, gain_ref, wq_ref, wkv_ref, wo_ref,
    out_ref, odocs_ref,
    state, gain, xg, w, wo, q, kv, dc, att,
    far, fwd, bwd, half_f, half_b, got_f, got_b, done,
    load_sem, xs_sem, xr_sem, dsend, drecv, ws_sem, wr_sem, kvs_sem, kvr_sem,
    wos_sem, wor_sem, ats_sem, atr_sem, rs_send, rs_recv, sh_send, sh_recv,
):
    width = state.shape[1]
    cw = width // NJ
    ww = width // NW
    sec = lax.axis_index("section")
    ten = lax.axis_index("tensor")
    nsec = lax.axis_size("section")
    xh, y, core = ten // (2 * YS), (ten // 2) % YS, ten % 2

    def at(dh, dy, dcore=0):
        return (sec, ((xh + dh) % 2) * (2 * YS) + ((y + dy) % YS) * 2 + (core + dcore) % 2)

    def block_of(dh, dy):
        return ((xh + dh) % 2) * YS + (y + dy) % YS

    twin, across, ahead, behind = at(0, 0, 1), at(1, 0), at(0, 1), at(0, 3)
    following = ((sec + 1) % nsec, ten)
    before = ((sec + nsec - 1) % nsec, ten)

    loads = [
        pltpu.make_async_copy(state_ref.at[0], state, load_sem.at[0]),
        pltpu.make_async_copy(gain_ref, gain, load_sem.at[1]),
        pltpu.make_async_copy(docs_ref, dc.at[PAD + 2 * block_of(0, 0) + core], load_sem.at[2]),
        pltpu.make_async_copy(wq_ref.at[0], w.at[core], load_sem.at[3]),
        pltpu.make_async_copy(
            wkv_ref.at[0], w.at[2, :, pl.ds(pl.multiple_of(core * HD, HD), HD)], load_sem.at[4]
        ),
        pltpu.make_async_copy(
            wo_ref.at[0], wo.at[0, pl.ds(pl.multiple_of(core * 256, 256), 256), :], load_sem.at[5]
        ),
    ]
    for copy in loads:
        copy.start()

    barrier = pltpu.get_barrier_semaphore()
    for other in (twin, across, ahead, behind, following, before):
        pl.semaphore_signal(barrier, inc=1, device_id=other, device_id_type=MESH)

    for index in range(PAD):
        kv[index] = jnp.zeros((BLK, 2 * HD), jnp.bfloat16)
        dc[index] = jnp.full((1, BLK), -1, jnp.int32)

    def remote(src, dst, send, recv, target):
        return pltpu.make_async_remote_copy(
            src_ref=src, dst_ref=dst, send_sem=send, recv_sem=recv, device_id=target, device_id_type=MESH
        )

    sent = []

    def go(copy):
        copy.start()
        sent.append(copy)
        return copy

    def piece(number, src, dst, part, target):
        rows = FIRST if part == 0 else SECOND
        return remote(
            xg.at[src, rows, :], xg.at[dst, rows, :], xs_sem.at[number], xr_sem.at[dst, part], target
        )

    def arrived(slot, part):
        rows = FIRST if part == 0 else SECOND
        remote(
            xg.at[slot, rows, :], xg.at[slot, rows, :], xs_sem.at[0], xr_sem.at[slot, part], twin
        ).wait_recv()

    def doc_pair(dh, dy):
        return dc.at[pl.ds(PAD + 2 * block_of(dh, dy), 2)]

    def send_docs(number, dh, dy, recv, target):
        ref = doc_pair(dh, dy)
        return remote(ref, ref, dsend.at[number], drecv.at[recv], target)

    def docs_arrived(recv, dh, dy):
        ref = doc_pair(dh, dy)
        remote(ref, ref, dsend.at[0], drecv.at[recv], twin).wait_recv()

    loads[0].wait()
    loads[1].wait()

    def norm(rows):
        wide = state[rows, :].astype(jnp.float32)
        factor = lax.rsqrt(jnp.mean(wide * wide, axis=-1, keepdims=True) + 1e-05)
        xg[OWN, rows, :] = (wide * factor * gain[...]).astype(jnp.bfloat16)

    norm(FIRST)
    pl.semaphore_wait(barrier, 6)
    go(piece(0, OWN, BEHIND, 0, ahead))
    across_first = piece(1, OWN, ACROSS, 0, across)
    across_first.start()
    norm(SECOND)
    go(piece(2, OWN, AHEAD, 1, behind))
    go(piece(3, OWN, BEHIND, 1, ahead))
    go(piece(4, OWN, AHEAD, 0, behind))

    loads[2].wait()
    own_docs = dc.at[PAD + 2 * block_of(0, 0) + core]
    go(remote(own_docs, own_docs, dsend.at[0], drecv.at[0], twin))
    go(remote(docs_ref, odocs_ref, dsend.at[9], drecv.at[9], following))
    go(remote(wq_ref.at[0], w.at[core], ws_sem.at[0], wr_sem.at[0], twin))
    kv_cols = w.at[2, :, pl.ds(pl.multiple_of(core * HD, HD), HD)]
    go(remote(wkv_ref.at[0], kv_cols, ws_sem.at[1], wr_sem.at[1], twin))
    twin_docs = dc.at[PAD + 2 * block_of(0, 0) + 1 - core]
    remote(twin_docs, twin_docs, dsend.at[0], drecv.at[0], twin).wait_recv()
    go(send_docs(1, 0, 0, 1, across))
    go(send_docs(2, 0, 0, 2, ahead))
    go(send_docs(3, 0, 0, 3, behind))

    def project(slot, count):
        rows = xg[pl.ds(slot, count)].reshape(count * BLK, width)
        for index in (2, 0, 1):
            res = jnp.dot(rows, w[index], preferred_element_type=jnp.float32).astype(jnp.bfloat16)
            for one in range(count):
                dh, dy = SLOTS[slot + one]
                part = res[one * BLK : (one + 1) * BLK]
                if index < 2:
                    q[dh * YS + dy, 2 * index] = part[:, :HD]
                    q[dh * YS + dy, 2 * index + 1] = part[:, HD:]
                else:
                    ref = kv.at[PAD + 2 * block_of(dh, dy) + core]
                    ref[...] = part
                    go(remote(ref, ref, kvs_sem.at[slot + one], kvr_sem.at[slot + one], twin))

    def wo_piece(chunk):
        return pl.ds(chunk * ww, ww)

    def wo_across(chunk):
        dst = wo.at[1, pl.ds(pl.multiple_of(core * 256, 256), 256), wo_piece(chunk)]
        return remote(wo_ref.at[0, :, wo_piece(chunk)], dst, wos_sem.at[chunk], wor_sem.at[chunk], across)

    def wo_relay(chunk):
        ref = wo.at[1, pl.ds(pl.multiple_of(core * 256, 256), 256), wo_piece(chunk)]
        return remote(ref, ref, wos_sem.at[NW + chunk], wor_sem.at[NW + chunk], twin)

    def pass_wo(chunk):
        wo_across(chunk).wait_recv()
        go(wo_relay(chunk))

    across_first.wait_send()
    across_last = piece(5, OWN, ACROSS, 1, across)
    across_last.start()
    arrived(ACROSS, 0)
    go(piece(8, ACROSS, BEHIND2, 0, ahead))
    go(piece(10, ACROSS, AHEAD2, 0, behind))
    arrived(ACROSS, 1)
    go(piece(9, ACROSS, AHEAD2, 1, behind))
    last_ahead = piece(11, ACROSS, BEHIND2, 1, ahead)
    last_ahead.start()
    across_last.wait_send()
    for chunk in range(3):
        go(wo_across(chunk))
    docs_arrived(1, 1, 0)
    go(send_docs(4, 1, 0, 4, ahead))
    go(send_docs(5, 1, 0, 5, behind))
    docs_arrived(2, 0, 3)
    go(send_docs(6, 0, 3, 6, ahead))
    docs_arrived(3, 0, 1)
    go(remote(
        wo_ref.at[0], wo.at[0, pl.ds(pl.multiple_of(core * 256, 256), 256), :],
        wos_sem.at[2 * NW], wor_sem.at[2 * NW], twin,
    ))

    for copy in loads[3:]:
        copy.wait()
    remote(w.at[1 - core], w.at[1 - core], ws_sem.at[0], wr_sem.at[0], twin).wait_recv()
    kv_cols2 = w.at[2, :, pl.ds(pl.multiple_of((1 - core) * HD, HD), HD)]
    remote(kv_cols2, kv_cols2, ws_sem.at[1], wr_sem.at[1], twin).wait_recv()
    project(OWN, 2)
    docs_arrived(4, 1, 3)
    go(send_docs(7, 1, 3, 7, ahead))
    docs_arrived(5, 1, 1)
    def twin_keys(slots):
        for slot in slots:
            dh, dy = SLOTS[slot]
            ref = kv.at[PAD + 2 * block_of(dh, dy) + 1 - core]
            remote(ref, ref, kvs_sem.at[slot], kvr_sem.at[slot], twin).wait_recv()

    factor = HD ** (-0.5) * LOG2E

    def attend(dh, dy):
        block = 2 * block_of(dh, dy) + core
        heads = q[dh * YS + dy].reshape(4 * BLK, HD)
        keys = kv[pl.ds(block, WIN), :, :HD].reshape(WIN * BLK, HD)
        values = kv[pl.ds(block, WIN), :, HD:].reshape(WIN * BLK, HD)
        scores = lax.dot_general(
            heads, keys, (((1,), (1,)), ((), ())), preferred_element_type=jnp.float32
        ).reshape(4, BLK, WIN * BLK)
        key_docs = dc[pl.ds(block, WIN)].astype(jnp.float32)
        row_docs = jnp.broadcast_to(key_docs[WIN - 1], (BLK, BLK)).T
        tiles = []
        for index in range(WIN):
            same = row_docs == key_docs[index]
            if index == WIN - 1:
                same = same & (
                    lax.broadcasted_iota(jnp.int32, (BLK, BLK), 1)
                    <= lax.broadcasted_iota(jnp.int32, (BLK, BLK), 0)
                )
            tiles.append(
                jnp.where(same[None], scores[:, :, index * BLK : (index + 1) * BLK], -jnp.inf)
            )
        top = functools.reduce(jnp.maximum, tiles)
        top = jnp.max(top, axis=-1, keepdims=True) * factor
        tiles = [jnp.exp2(tile * factor - top) for tile in tiles]
        total = jnp.sum(functools.reduce(jnp.add, tiles), axis=-1, keepdims=True)
        probs = jnp.concatenate([tile.astype(jnp.bfloat16) for tile in tiles], axis=-1)
        res = jnp.dot(
            probs.reshape(4 * BLK, WIN * BLK), values, preferred_element_type=jnp.float32
        ).reshape(4, BLK, HD)
        return (res / total).astype(jnp.bfloat16)

    def att_copy(place):
        return remote(att.at[2, place], att.at[1, place], ats_sem.at[place], atr_sem.at[place], across)

    def attend_all(order):
        def one(i, carry):
            code = jnp.int32(order[-1])
            for index in range(len(order) - 1):
                code = jnp.where(i == index, order[index], code)
            dh, place = code // YS, code % YS
            dy = jnp.where(place < 2, 2 - place, 9 - 3 * place)
            res = attend(dh, dy)
            for head in range(4):
                att[2 * dh, place, :, head * HD : (head + 1) * HD] = res[head]

            @pl.when(dh == 1)
            def _():
                att_copy(place).start()

            return carry

        lax.fori_loop(0, len(order), one, 0)

    for slot in (BEHIND, AHEAD):
        for part in range(2):
            arrived(slot, part)
    go(wo_across(3))
    arrived(BEHIND2, 0)
    go(piece(12, BEHIND2, FAR2, 0, ahead))
    arrived(AHEAD2, 1)
    go(piece(13, AHEAD2, FAR2, 1, behind))
    last_ahead.wait_send()
    go(piece(6, BEHIND, FAR, 0, ahead))
    go(piece(7, AHEAD, FAR, 1, behind))
    go(wo_across(4))
    project(BEHIND, 2)
    pass_wo(0)
    arrived(BEHIND2, 1)
    arrived(AHEAD2, 0)
    project(BEHIND2, 2)
    pass_wo(1)
    docs_arrived(6, 0, 2)
    docs_arrived(7, 1, 2)
    arrived(FAR2, 0)
    arrived(FAR2, 1)
    project(FAR2, 1)
    twin_keys((OWN, ACROSS, BEHIND, AHEAD, BEHIND2, AHEAD2, FAR2))
    attend_all((4, 5, 1))
    pass_wo(2)
    pass_wo(3)
    arrived(FAR, 0)
    arrived(FAR, 1)
    project(FAR, 1)
    twin_keys((FAR,))
    attend_all((0,))
    pass_wo(4)
    own_wo = wo.at[0, pl.ds(pl.multiple_of((1 - core) * 256, 256), 256), :]
    remote(own_wo, own_wo, wos_sem.at[2 * NW], wor_sem.at[2 * NW], twin).wait_recv()
    att_copy(0).wait_recv()

    def half_copies(k):
        return (
            remote(far.at[k, FIRST, :], half_f.at[k], rs_send.at[0, k], rs_recv.at[0, k], ahead),
            remote(far.at[k, SECOND, :], half_b.at[k], rs_send.at[1, k], rs_recv.at[1, k], behind),
        )

    def full_copies(k):
        return (
            remote(fwd.at[k], got_f.at[k], rs_send.at[2, k], rs_recv.at[2, k], ahead),
            remote(bwd.at[k], got_b.at[k], rs_send.at[3, k], rs_recv.at[3, k], behind),
        )

    def cols(k):
        return pl.ds(pl.multiple_of(k * cw, cw), cw)

    def shift_copy(k):
        return remote(done.at[k], out_ref.at[0, :, cols(k)], sh_send.at[k], sh_recv.at[k], following)

    def product(first, count, k):
        return sum(
            jnp.dot(
                att[group, pl.ds(first, count)].reshape(count * BLK, 4 * HD),
                wo[group, :, cols(k)],
                preferred_element_type=jnp.float32,
            )
            for group in range(2)
        )

    def far_step(i, carry):
        for chunk in range(NW):
            @pl.when(i == chunk * (NJ // NW))
            def _():
                ref = wo.at[1, pl.ds(pl.multiple_of((1 - core) * 256, 256), 256), wo_piece(chunk)]
                remote(
                    ref, ref, wos_sem.at[NW + chunk], wor_sem.at[NW + chunk], twin
                ).wait_recv()

        far[i] = product(0, 1, i).astype(jnp.bfloat16)
        for copy in half_copies(i):
            copy.start()
        return carry

    lax.fori_loop(0, NJ, far_step, 0)
    attend_all((6, 7, 2, 3))
    att_copy(1).wait_recv()
    att_copy(2).wait_recv()

    def step(i, carry):
        @pl.when(i < NJ)
        def _():
            res = product(1, 2, i)
            first, second = half_copies(i)
            to_f, to_b = full_copies(i)
            first.wait_recv()
            fwd[i, SECOND, :] = res[HALF:BLK].astype(jnp.bfloat16)
            fwd[i, FIRST, :] = (res[:HALF] + half_f[i].astype(jnp.float32)).astype(jnp.bfloat16)
            to_f.start()
            second.wait_recv()
            bwd[i, FIRST, :] = res[BLK : BLK + HALF].astype(jnp.bfloat16)
            bwd[i, SECOND, :] = (res[BLK + HALF :] + half_b[i].astype(jnp.float32)).astype(jnp.bfloat16)
            to_b.start()

        @pl.when(i == LAG)
        def _():
            att_copy(3).wait_recv()

        @pl.when(i >= LAG)
        def _():
            k = i - LAG
            total = state[:, cols(k)].astype(jnp.float32) + product(3, 1, k)
            from_b, from_f = full_copies(k)
            from_b.wait_recv()
            from_f.wait_recv()
            total = total + got_f[k].astype(jnp.float32) + got_b[k].astype(jnp.float32)
            done[k] = total.astype(jnp.bfloat16)
            shift_copy(k).start()

        return carry

    lax.fori_loop(0, NJ + LAG, step, 0)

    for copy in sent:
        copy.wait_send()
    for place in range(YS):
        att_copy(place).wait_send()

    def finish(k, carry):
        for copy in half_copies(k) + full_copies(k):
            copy.wait_send()
        shift_copy(k).wait()
        return carry

    lax.fori_loop(0, NJ, finish, 0)
    remote(docs_ref, odocs_ref, dsend.at[9], drecv.at[9], following).wait_recv()


def local(state, docs, gain, w_query, w_keyval, w_out):
    width = state.shape[2]
    cw = width // NJ
    bf, f32 = jnp.bfloat16, jnp.float32
    dma = pltpu.SemaphoreType.DMA
    anyspace = pl.BlockSpec(memory_space=pl.ANY)
    return tuple(pl.pallas_call(
        body,
        out_shape=(
            jax.ShapeDtypeStruct(state.shape, state.dtype),
            jax.ShapeDtypeStruct(docs.shape, docs.dtype),
        ),
        in_specs=[anyspace] * 6,
        out_specs=(anyspace, anyspace),
        scratch_shapes=[
            pltpu.VMEM((BLK, width), bf),
            pltpu.VMEM((1, width), f32),
            pltpu.VMEM((8, BLK, width), bf),
            pltpu.VMEM((3, width, 2 * HD), bf),
            pltpu.VMEM((2, 4 * HD, width), bf),
            pltpu.VMEM((8, 4, BLK, HD), bf),
            pltpu.VMEM((16 + PAD, BLK, 2 * HD), bf),
            pltpu.VMEM((16 + PAD, 1, BLK), jnp.int32),
            pltpu.VMEM((3, YS, BLK, 4 * HD), bf),
            pltpu.VMEM((NJ, BLK, cw), bf),
            pltpu.VMEM((NJ, BLK, cw), bf),
            pltpu.VMEM((NJ, BLK, cw), bf),
            pltpu.VMEM((NJ, HALF, cw), bf),
            pltpu.VMEM((NJ, HALF, cw), bf),
            pltpu.VMEM((NJ, BLK, cw), bf),
            pltpu.VMEM((NJ, BLK, cw), bf),
            pltpu.VMEM((NJ, BLK, cw), bf),
            dma((6,)),
            dma((14,)), dma((8, 2)),
            dma((10,)), dma((10,)),
            dma((2,)), dma((2,)),
            dma((8,)), dma((8,)),
            dma((2 * NW + 1,)), dma((2 * NW + 1,)),
            dma((YS,)), dma((YS,)),
            dma((4, NJ)), dma((4, NJ)),
            dma((NJ,)), dma((NJ,)),
        ],
        compiler_params=pltpu.CompilerParams(
            collective_id=0, has_side_effects=True, vmem_limit_bytes=52 << 20
        ),
        name="layer",
    )(state, docs, gain, w_query, w_keyval, w_out))


def solution(mesh):
    in_specs = (
        P("section", "tensor", None),
        P("section", "tensor"),
        P("section", None),
        P("section", None, "tensor"),
        P("section", None, "tensor"),
        P("section", "tensor", None),
    )
    out_specs = (P("section", "tensor", None), P("section", "tensor"))
    return jax.shard_map(local, mesh=mesh, in_specs=in_specs, out_specs=out_specs, check_vma=False)
```

```python
import functools

import jax
import jax.numpy as jnp
from jax import lax
from jax.experimental import pallas as pl
from jax.experimental.pallas import tpu as pltpu
from jax.sharding import PartitionSpec as P

MESH = pl.DeviceIdType.MESH
BLK = 128
HALF = 64
HD = 128
WIN = 5
PAD = WIN - 1
YS = 4
NJ = 20
EARLY = 6
LAG = 7
NW = 5
SLOTS = ((0, 0), (1, 0), (0, 3), (0, 1), (1, 3), (1, 1), (0, 2), (1, 2))
OWN, ACROSS, BEHIND, AHEAD, BEHIND2, AHEAD2, FAR, FAR2 = range(8)
LOG2E = 1.4426950408889634
FIRST = pl.ds(0, HALF)
SECOND = pl.ds(HALF, HALF)


def body(
    state_ref, docs_ref, gain_ref, wq_ref, wkv_ref, wo_ref,
    out_ref, odocs_ref,
    state, gain, xg, w, wo, q, kv, dc, att,
    far, fwd, bwd, half_f, half_b, got_f, got_b, done,
    load_sem, xs_sem, xr_sem, dsend, drecv, ws_sem, wr_sem, kvs_sem, kvr_sem,
    wos_sem, wor_sem, ats_sem, atr_sem, rs_send, rs_recv, sh_send, sh_recv,
):
    width = state.shape[1]
    cw = width // NJ
    ww = width // NW
    sec = lax.axis_index("section")
    ten = lax.axis_index("tensor")
    nsec = lax.axis_size("section")
    xh, y, core = ten // (2 * YS), (ten // 2) % YS, ten % 2

    def at(dh, dy, dcore=0):
        return (sec, ((xh + dh) % 2) * (2 * YS) + ((y + dy) % YS) * 2 + (core + dcore) % 2)

    def block_of(dh, dy):
        return ((xh + dh) % 2) * YS + (y + dy) % YS

    twin, across, ahead, behind = at(0, 0, 1), at(1, 0), at(0, 1), at(0, 3)
    following = ((sec + 1) % nsec, ten)
    before = ((sec + nsec - 1) % nsec, ten)

    loads = [
        pltpu.make_async_copy(state_ref.at[0], state, load_sem.at[0]),
        pltpu.make_async_copy(gain_ref, gain, load_sem.at[1]),
        pltpu.make_async_copy(docs_ref, dc.at[PAD + 2 * block_of(0, 0) + core], load_sem.at[2]),
        pltpu.make_async_copy(wq_ref.at[0], w.at[core], load_sem.at[3]),
        pltpu.make_async_copy(
            wkv_ref.at[0], w.at[2, :, pl.ds(pl.multiple_of(core * HD, HD), HD)], load_sem.at[4]
        ),
        pltpu.make_async_copy(
            wo_ref.at[0], wo.at[0, pl.ds(pl.multiple_of(core * 256, 256), 256), :], load_sem.at[5]
        ),
    ]
    for copy in loads:
        copy.start()

    barrier = pltpu.get_barrier_semaphore()
    for other in (twin, across, ahead, behind, following, before):
        pl.semaphore_signal(barrier, inc=1, device_id=other, device_id_type=MESH)

    for index in range(PAD):
        kv[index] = jnp.zeros((BLK, 2 * HD), jnp.bfloat16)
        dc[index] = jnp.full((1, BLK), -1, jnp.int32)

    def remote(src, dst, send, recv, target):
        return pltpu.make_async_remote_copy(
            src_ref=src, dst_ref=dst, send_sem=send, recv_sem=recv, device_id=target, device_id_type=MESH
        )

    sent = []

    def go(copy):
        copy.start()
        sent.append(copy)
        return copy

    def piece(number, src, dst, part, target):
        rows = FIRST if part == 0 else SECOND
        return remote(
            xg.at[src, rows, :], xg.at[dst, rows, :], xs_sem.at[number], xr_sem.at[dst, part], target
        )

    def arrived(slot, part):
        rows = FIRST if part == 0 else SECOND
        remote(
            xg.at[slot, rows, :], xg.at[slot, rows, :], xs_sem.at[0], xr_sem.at[slot, part], twin
        ).wait_recv()

    def doc_pair(dh, dy):
        return dc.at[pl.ds(PAD + 2 * block_of(dh, dy), 2)]

    def send_docs(number, dh, dy, recv, target):
        ref = doc_pair(dh, dy)
        return remote(ref, ref, dsend.at[number], drecv.at[recv], target)

    def docs_arrived(recv, dh, dy):
        ref = doc_pair(dh, dy)
        remote(ref, ref, dsend.at[0], drecv.at[recv], twin).wait_recv()

    loads[0].wait()
    loads[1].wait()

    def norm(rows):
        wide = state[rows, :].astype(jnp.float32)
        factor = lax.rsqrt(jnp.mean(wide * wide, axis=-1, keepdims=True) + 1e-05)
        xg[OWN, rows, :] = (wide * factor * gain[...]).astype(jnp.bfloat16)

    norm(FIRST)
    pl.semaphore_wait(barrier, 6)
    go(piece(0, OWN, BEHIND, 0, ahead))
    across_first = piece(1, OWN, ACROSS, 0, across)
    across_first.start()
    norm(SECOND)
    go(piece(2, OWN, AHEAD, 1, behind))
    go(piece(3, OWN, BEHIND, 1, ahead))
    go(piece(4, OWN, AHEAD, 0, behind))

    loads[2].wait()
    own_docs = dc.at[PAD + 2 * block_of(0, 0) + core]
    go(remote(own_docs, own_docs, dsend.at[0], drecv.at[0], twin))
    go(remote(docs_ref, odocs_ref, dsend.at[9], drecv.at[9], following))
    go(remote(wq_ref.at[0], w.at[core], ws_sem.at[0], wr_sem.at[0], twin))
    kv_cols = w.at[2, :, pl.ds(pl.multiple_of(core * HD, HD), HD)]
    go(remote(wkv_ref.at[0], kv_cols, ws_sem.at[1], wr_sem.at[1], twin))
    twin_docs = dc.at[PAD + 2 * block_of(0, 0) + 1 - core]
    remote(twin_docs, twin_docs, dsend.at[0], drecv.at[0], twin).wait_recv()
    go(send_docs(1, 0, 0, 1, across))
    go(send_docs(2, 0, 0, 2, ahead))
    go(send_docs(3, 0, 0, 3, behind))

    def project(slot, count):
        rows = xg[pl.ds(slot, count)].reshape(count * BLK, width)
        for index in (2, 0, 1):
            res = jnp.dot(rows, w[index], preferred_element_type=jnp.float32).astype(jnp.bfloat16)
            for one in range(count):
                dh, dy = SLOTS[slot + one]
                part = res[one * BLK : (one + 1) * BLK]
                if index < 2:
                    q[dh * YS + dy, 2 * index] = part[:, :HD]
                    q[dh * YS + dy, 2 * index + 1] = part[:, HD:]
                else:
                    ref = kv.at[PAD + 2 * block_of(dh, dy) + core]
                    ref[...] = part
                    go(remote(ref, ref, kvs_sem.at[slot + one], kvr_sem.at[slot + one], twin))

    def wo_piece(chunk):
        return pl.ds(chunk * ww, ww)

    def wo_across(chunk):
        dst = wo.at[1, pl.ds(pl.multiple_of(core * 256, 256), 256), wo_piece(chunk)]
        return remote(wo_ref.at[0, :, wo_piece(chunk)], dst, wos_sem.at[chunk], wor_sem.at[chunk], across)

    def wo_relay(chunk):
        ref = wo.at[1, pl.ds(pl.multiple_of(core * 256, 256), 256), wo_piece(chunk)]
        return remote(ref, ref, wos_sem.at[NW + chunk], wor_sem.at[NW + chunk], twin)

    def pass_wo(chunk):
        wo_across(chunk).wait_recv()
        go(wo_relay(chunk))

    across_first.wait_send()
    across_last = piece(5, OWN, ACROSS, 1, across)
    across_last.start()
    arrived(ACROSS, 0)
    go(piece(8, ACROSS, BEHIND2, 0, ahead))
    go(piece(10, ACROSS, AHEAD2, 0, behind))
    arrived(ACROSS, 1)
    go(piece(9, ACROSS, AHEAD2, 1, behind))
    last_ahead = piece(11, ACROSS, BEHIND2, 1, ahead)
    last_ahead.start()
    across_last.wait_send()
    for chunk in range(3):
        go(wo_across(chunk))
    docs_arrived(1, 1, 0)
    go(send_docs(4, 1, 0, 4, ahead))
    go(send_docs(5, 1, 0, 5, behind))
    docs_arrived(2, 0, 3)
    go(send_docs(6, 0, 3, 6, ahead))
    docs_arrived(3, 0, 1)
    go(remote(
        wo_ref.at[0], wo.at[0, pl.ds(pl.multiple_of(core * 256, 256), 256), :],
        wos_sem.at[2 * NW], wor_sem.at[2 * NW], twin,
    ))

    for copy in loads[3:]:
        copy.wait()
    remote(w.at[1 - core], w.at[1 - core], ws_sem.at[0], wr_sem.at[0], twin).wait_recv()
    kv_cols2 = w.at[2, :, pl.ds(pl.multiple_of((1 - core) * HD, HD), HD)]
    remote(kv_cols2, kv_cols2, ws_sem.at[1], wr_sem.at[1], twin).wait_recv()
    project(OWN, 2)
    docs_arrived(4, 1, 3)
    go(send_docs(7, 1, 3, 7, ahead))
    docs_arrived(5, 1, 1)
    def twin_keys(slots):
        for slot in slots:
            dh, dy = SLOTS[slot]
            ref = kv.at[PAD + 2 * block_of(dh, dy) + 1 - core]
            remote(ref, ref, kvs_sem.at[slot], kvr_sem.at[slot], twin).wait_recv()

    factor = HD ** (-0.5) * LOG2E

    def attend(dh, dy):
        block = 2 * block_of(dh, dy) + core
        heads = q[dh * YS + dy].reshape(4 * BLK, HD)
        keys = kv[pl.ds(block, WIN), :, :HD].reshape(WIN * BLK, HD)
        values = kv[pl.ds(block, WIN), :, HD:].reshape(WIN * BLK, HD)
        scores = lax.dot_general(
            heads, keys, (((1,), (1,)), ((), ())), preferred_element_type=jnp.float32
        ).reshape(4, BLK, WIN * BLK)
        key_docs = dc[pl.ds(block, WIN)].astype(jnp.float32)
        row_docs = jnp.broadcast_to(key_docs[WIN - 1], (BLK, BLK)).T
        tiles = []
        for index in range(WIN):
            same = row_docs == key_docs[index]
            if index == WIN - 1:
                same = same & (
                    lax.broadcasted_iota(jnp.int32, (BLK, BLK), 1)
                    <= lax.broadcasted_iota(jnp.int32, (BLK, BLK), 0)
                )
            tiles.append(
                jnp.where(same[None], scores[:, :, index * BLK : (index + 1) * BLK], -jnp.inf)
            )
        top = functools.reduce(jnp.maximum, tiles)
        top = jnp.max(top, axis=-1, keepdims=True) * factor
        tiles = [jnp.exp2(tile * factor - top) for tile in tiles]
        total = jnp.sum(functools.reduce(jnp.add, tiles), axis=-1, keepdims=True)
        probs = jnp.concatenate([tile.astype(jnp.bfloat16) for tile in tiles], axis=-1)
        res = jnp.dot(
            probs.reshape(4 * BLK, WIN * BLK), values, preferred_element_type=jnp.float32
        ).reshape(4, BLK, HD)
        return (res / total).astype(jnp.bfloat16)

    def att_copy(place):
        return remote(att.at[2, place], att.at[1, place], ats_sem.at[place], atr_sem.at[place], across)

    def attend_all(order):
        def one(i, carry):
            code = jnp.int32(order[-1])
            for index in range(len(order) - 1):
                code = jnp.where(i == index, order[index], code)
            dh, place = code // YS, code % YS
            dy = jnp.where(place < 2, 2 - place, 9 - 3 * place)
            res = attend(dh, dy)
            for head in range(4):
                att[2 * dh, place, :, head * HD : (head + 1) * HD] = res[head]

            @pl.when(dh == 1)
            def _():
                att_copy(place).start()

            return carry

        lax.fori_loop(0, len(order), one, 0)

    for slot in (BEHIND, AHEAD):
        for part in range(2):
            arrived(slot, part)
    go(wo_across(3))
    arrived(BEHIND2, 0)
    go(piece(12, BEHIND2, FAR2, 0, ahead))
    arrived(AHEAD2, 1)
    go(piece(13, AHEAD2, FAR2, 1, behind))
    last_ahead.wait_send()
    go(piece(6, BEHIND, FAR, 0, ahead))
    go(piece(7, AHEAD, FAR, 1, behind))
    go(wo_across(4))
    project(BEHIND, 2)
    pass_wo(0)
    arrived(BEHIND2, 1)
    arrived(AHEAD2, 0)
    project(BEHIND2, 2)
    pass_wo(1)
    docs_arrived(6, 0, 2)
    docs_arrived(7, 1, 2)
    arrived(FAR2, 0)
    arrived(FAR2, 1)
    project(FAR2, 1)
    twin_keys((OWN, ACROSS, BEHIND, AHEAD, BEHIND2, AHEAD2, FAR2))
    attend_all((4, 5, 1))
    pass_wo(2)
    pass_wo(3)
    arrived(FAR, 0)
    arrived(FAR, 1)
    project(FAR, 1)
    twin_keys((FAR,))
    attend_all((0,))
    pass_wo(4)
    own_wo = wo.at[0, pl.ds(pl.multiple_of((1 - core) * 256, 256), 256), :]
    remote(own_wo, own_wo, wos_sem.at[2 * NW], wor_sem.at[2 * NW], twin).wait_recv()
    att_copy(0).wait_recv()

    def half_copies(k):
        return (
            remote(far.at[k, FIRST, :], half_f.at[k], rs_send.at[0, k], rs_recv.at[0, k], ahead),
            remote(far.at[k, SECOND, :], half_b.at[k], rs_send.at[1, k], rs_recv.at[1, k], behind),
        )

    def full_copies(k):
        return (
            remote(fwd.at[k], got_f.at[k], rs_send.at[2, k], rs_recv.at[2, k], ahead),
            remote(bwd.at[k], got_b.at[k], rs_send.at[3, k], rs_recv.at[3, k], behind),
        )

    def cols(k):
        return pl.ds(pl.multiple_of(k * cw, cw), cw)

    def shift_copy(k):
        return remote(done.at[k], out_ref.at[0, :, cols(k)], sh_send.at[k], sh_recv.at[k], following)

    def product(first, count, k):
        return sum(
            jnp.dot(
                att[group, pl.ds(first, count)].reshape(count * BLK, 4 * HD),
                wo[group, :, cols(k)],
                preferred_element_type=jnp.float32,
            )
            for group in range(2)
        )

    def far_step(i, carry):
        for chunk in range(NW):
            @pl.when(i == chunk * (NJ // NW))
            def _():
                ref = wo.at[1, pl.ds(pl.multiple_of((1 - core) * 256, 256), 256), wo_piece(chunk)]
                remote(
                    ref, ref, wos_sem.at[NW + chunk], wor_sem.at[NW + chunk], twin
                ).wait_recv()

        far[i] = product(0, 1, i).astype(jnp.bfloat16)
        for copy in half_copies(i):
            copy.start()
        return carry

    lax.fori_loop(0, EARLY, far_step, 0)
    attend_all((6, 7))
    lax.fori_loop(EARLY, NJ, far_step, 0)
    attend_all((2, 3))
    att_copy(1).wait_recv()
    att_copy(2).wait_recv()

    def step(i, carry):
        @pl.when(i < NJ)
        def _():
            res = product(1, 2, i)
            first, second = half_copies(i)
            to_f, to_b = full_copies(i)
            first.wait_recv()
            fwd[i, SECOND, :] = res[HALF:BLK].astype(jnp.bfloat16)
            fwd[i, FIRST, :] = (res[:HALF] + half_f[i].astype(jnp.float32)).astype(jnp.bfloat16)
            to_f.start()
            second.wait_recv()
            bwd[i, FIRST, :] = res[BLK : BLK + HALF].astype(jnp.bfloat16)
            bwd[i, SECOND, :] = (res[BLK + HALF :] + half_b[i].astype(jnp.float32)).astype(jnp.bfloat16)
            to_b.start()

        @pl.when(i == LAG)
        def _():
            att_copy(3).wait_recv()

        @pl.when(i >= LAG)
        def _():
            k = i - LAG
            total = state[:, cols(k)].astype(jnp.float32) + product(3, 1, k)
            from_b, from_f = full_copies(k)
            from_b.wait_recv()
            from_f.wait_recv()
            total = total + got_f[k].astype(jnp.float32) + got_b[k].astype(jnp.float32)
            done[k] = total.astype(jnp.bfloat16)
            shift_copy(k).start()

        return carry

    lax.fori_loop(0, NJ + LAG, step, 0)

    for copy in sent:
        copy.wait_send()
    for place in range(YS):
        att_copy(place).wait_send()

    def finish(k, carry):
        for copy in half_copies(k) + full_copies(k):
            copy.wait_send()
        shift_copy(k).wait()
        return carry

    lax.fori_loop(0, NJ, finish, 0)
    remote(docs_ref, odocs_ref, dsend.at[9], drecv.at[9], following).wait_recv()


def local(state, docs, gain, w_query, w_keyval, w_out):
    width = state.shape[2]
    cw = width // NJ
    bf, f32 = jnp.bfloat16, jnp.float32
    dma = pltpu.SemaphoreType.DMA
    anyspace = pl.BlockSpec(memory_space=pl.ANY)
    return tuple(pl.pallas_call(
        body,
        out_shape=(
            jax.ShapeDtypeStruct(state.shape, state.dtype),
            jax.ShapeDtypeStruct(docs.shape, docs.dtype),
        ),
        in_specs=[anyspace] * 6,
        out_specs=(anyspace, anyspace),
        scratch_shapes=[
            pltpu.VMEM((BLK, width), bf),
            pltpu.VMEM((1, width), f32),
            pltpu.VMEM((8, BLK, width), bf),
            pltpu.VMEM((3, width, 2 * HD), bf),
            pltpu.VMEM((2, 4 * HD, width), bf),
            pltpu.VMEM((8, 4, BLK, HD), bf),
            pltpu.VMEM((16 + PAD, BLK, 2 * HD), bf),
            pltpu.VMEM((16 + PAD, 1, BLK), jnp.int32),
            pltpu.VMEM((3, YS, BLK, 4 * HD), bf),
            pltpu.VMEM((NJ, BLK, cw), bf),
            pltpu.VMEM((NJ, BLK, cw), bf),
            pltpu.VMEM((NJ, BLK, cw), bf),
            pltpu.VMEM((NJ, HALF, cw), bf),
            pltpu.VMEM((NJ, HALF, cw), bf),
            pltpu.VMEM((NJ, BLK, cw), bf),
            pltpu.VMEM((NJ, BLK, cw), bf),
            pltpu.VMEM((NJ, BLK, cw), bf),
            dma((6,)),
            dma((14,)), dma((8, 2)),
            dma((10,)), dma((10,)),
            dma((2,)), dma((2,)),
            dma((8,)), dma((8,)),
            dma((2 * NW + 1,)), dma((2 * NW + 1,)),
            dma((YS,)), dma((YS,)),
            dma((4, NJ)), dma((4, NJ)),
            dma((NJ,)), dma((NJ,)),
        ],
        compiler_params=pltpu.CompilerParams(
            collective_id=0, has_side_effects=True, vmem_limit_bytes=52 << 20
        ),
        name="layer",
    )(state, docs, gain, w_query, w_keyval, w_out))


def solution(mesh):
    in_specs = (
        P("section", "tensor", None),
        P("section", "tensor"),
        P("section", None),
        P("section", None, "tensor"),
        P("section", None, "tensor"),
        P("section", "tensor", None),
    )
    out_specs = (P("section", "tensor", None), P("section", "tensor"))
    return jax.shard_map(local, mesh=mesh, in_specs=in_specs, out_specs=out_specs, check_vma=False)
```

```python
import functools

import jax
import jax.numpy as jnp
from jax import lax
from jax.experimental import pallas as pl
from jax.experimental.pallas import tpu as pltpu
from jax.sharding import PartitionSpec as P

MESH = pl.DeviceIdType.MESH
BLK = 128
HALF = 64
HD = 128
WIN = 5
PAD = WIN - 1
YS = 4
NJ = 20
LAG = 7
NW = 5
SLOTS = ((0, 0), (1, 0), (0, 3), (0, 1), (1, 3), (1, 1), (0, 2), (1, 2))
OWN, ACROSS, BEHIND, AHEAD, BEHIND2, AHEAD2, FAR, FAR2 = range(8)
LOG2E = 1.4426950408889634
FIRST = pl.ds(0, HALF)
SECOND = pl.ds(HALF, HALF)


def body(
    state_ref, docs_ref, gain_ref, wq_ref, wkv_ref, wo_ref,
    out_ref, odocs_ref,
    state, gain, xg, w, wo, q, kv, dc, att,
    far, fwd, bwd, half_f, half_b, got_f, got_b, done,
    load_sem, xs_sem, xr_sem, dsend, drecv, ws_sem, wr_sem, kvs_sem, kvr_sem,
    wos_sem, wor_sem, ats_sem, atr_sem, rs_send, rs_recv, sh_send, sh_recv,
):
    width = state.shape[1]
    cw = width // NJ
    ww = width // NW
    sec = lax.axis_index("section")
    ten = lax.axis_index("tensor")
    nsec = lax.axis_size("section")
    xh, y, core = ten // (2 * YS), (ten // 2) % YS, ten % 2

    def at(dh, dy, dcore=0):
        return (sec, ((xh + dh) % 2) * (2 * YS) + ((y + dy) % YS) * 2 + (core + dcore) % 2)

    def block_of(dh, dy):
        return ((xh + dh) % 2) * YS + (y + dy) % YS

    twin, across, ahead, behind = at(0, 0, 1), at(1, 0), at(0, 1), at(0, 3)
    following = ((sec + 1) % nsec, ten)
    before = ((sec + nsec - 1) % nsec, ten)

    loads = [
        pltpu.make_async_copy(state_ref.at[0], state, load_sem.at[0]),
        pltpu.make_async_copy(gain_ref, gain, load_sem.at[1]),
        pltpu.make_async_copy(docs_ref, dc.at[PAD + 2 * block_of(0, 0) + core], load_sem.at[2]),
        pltpu.make_async_copy(wq_ref.at[0], w.at[core], load_sem.at[3]),
        pltpu.make_async_copy(
            wkv_ref.at[0], w.at[2, :, pl.ds(pl.multiple_of(core * HD, HD), HD)], load_sem.at[4]
        ),
        pltpu.make_async_copy(
            wo_ref.at[0], wo.at[0, pl.ds(pl.multiple_of(core * 256, 256), 256), :], load_sem.at[5]
        ),
    ]
    for copy in loads:
        copy.start()

    barrier = pltpu.get_barrier_semaphore()
    for other in (twin, across, ahead, behind, following, before):
        pl.semaphore_signal(barrier, inc=1, device_id=other, device_id_type=MESH)

    for index in range(PAD):
        kv[index] = jnp.zeros((BLK, 2 * HD), jnp.bfloat16)
        dc[index] = jnp.full((1, BLK), -1, jnp.int32)

    def remote(src, dst, send, recv, target):
        return pltpu.make_async_remote_copy(
            src_ref=src, dst_ref=dst, send_sem=send, recv_sem=recv, device_id=target, device_id_type=MESH
        )

    sent = []

    def go(copy):
        copy.start()
        sent.append(copy)
        return copy

    def piece(number, src, dst, part, target):
        rows = FIRST if part == 0 else SECOND
        return remote(
            xg.at[src, rows, :], xg.at[dst, rows, :], xs_sem.at[number], xr_sem.at[dst, part], target
        )

    def arrived(slot, part):
        rows = FIRST if part == 0 else SECOND
        remote(
            xg.at[slot, rows, :], xg.at[slot, rows, :], xs_sem.at[0], xr_sem.at[slot, part], twin
        ).wait_recv()

    def doc_pair(dh, dy):
        return dc.at[pl.ds(PAD + 2 * block_of(dh, dy), 2)]

    def send_docs(number, dh, dy, recv, target):
        ref = doc_pair(dh, dy)
        return remote(ref, ref, dsend.at[number], drecv.at[recv], target)

    def docs_arrived(recv, dh, dy):
        ref = doc_pair(dh, dy)
        remote(ref, ref, dsend.at[0], drecv.at[recv], twin).wait_recv()

    loads[0].wait()
    loads[1].wait()

    def norm(rows):
        wide = state[rows, :].astype(jnp.float32)
        factor = lax.rsqrt(jnp.mean(wide * wide, axis=-1, keepdims=True) + 1e-05)
        xg[OWN, rows, :] = (wide * factor * gain[...]).astype(jnp.bfloat16)

    norm(FIRST)
    pl.semaphore_wait(barrier, 6)
    go(piece(0, OWN, BEHIND, 0, ahead))
    go(piece(4, OWN, AHEAD, 0, behind))
    across_first = piece(1, OWN, ACROSS, 0, across)
    across_first.start()
    norm(SECOND)
    go(piece(2, OWN, AHEAD, 1, behind))
    go(piece(3, OWN, BEHIND, 1, ahead))

    loads[2].wait()
    own_docs = dc.at[PAD + 2 * block_of(0, 0) + core]
    go(remote(own_docs, own_docs, dsend.at[0], drecv.at[0], twin))
    go(remote(docs_ref, odocs_ref, dsend.at[9], drecv.at[9], following))
    go(remote(wq_ref.at[0], w.at[core], ws_sem.at[0], wr_sem.at[0], twin))
    kv_cols = w.at[2, :, pl.ds(pl.multiple_of(core * HD, HD), HD)]
    go(remote(wkv_ref.at[0], kv_cols, ws_sem.at[1], wr_sem.at[1], twin))
    twin_docs = dc.at[PAD + 2 * block_of(0, 0) + 1 - core]
    remote(twin_docs, twin_docs, dsend.at[0], drecv.at[0], twin).wait_recv()
    go(send_docs(1, 0, 0, 1, across))
    go(send_docs(2, 0, 0, 2, ahead))
    go(send_docs(3, 0, 0, 3, behind))

    def project(slot, count):
        rows = xg[pl.ds(slot, count)].reshape(count * BLK, width)
        for index in (2, 0, 1):
            res = jnp.dot(rows, w[index], preferred_element_type=jnp.float32).astype(jnp.bfloat16)
            for one in range(count):
                dh, dy = SLOTS[slot + one]
                part = res[one * BLK : (one + 1) * BLK]
                if index < 2:
                    q[dh * YS + dy, 2 * index] = part[:, :HD]
                    q[dh * YS + dy, 2 * index + 1] = part[:, HD:]
                else:
                    ref = kv.at[PAD + 2 * block_of(dh, dy) + core]
                    ref[...] = part
                    go(remote(ref, ref, kvs_sem.at[slot + one], kvr_sem.at[slot + one], twin))

    def wo_piece(chunk):
        return pl.ds(chunk * ww, ww)

    def wo_across(chunk):
        dst = wo.at[1, pl.ds(pl.multiple_of(core * 256, 256), 256), wo_piece(chunk)]
        return remote(wo_ref.at[0, :, wo_piece(chunk)], dst, wos_sem.at[chunk], wor_sem.at[chunk], across)

    def wo_relay(chunk):
        ref = wo.at[1, pl.ds(pl.multiple_of(core * 256, 256), 256), wo_piece(chunk)]
        return remote(ref, ref, wos_sem.at[NW + chunk], wor_sem.at[NW + chunk], twin)

    def pass_wo(chunk):
        wo_across(chunk).wait_recv()
        go(wo_relay(chunk))

    across_first.wait_send()
    across_last = piece(5, OWN, ACROSS, 1, across)
    across_last.start()
    arrived(ACROSS, 0)
    go(piece(8, ACROSS, BEHIND2, 0, ahead))
    go(piece(10, ACROSS, AHEAD2, 0, behind))
    arrived(ACROSS, 1)
    go(piece(9, ACROSS, AHEAD2, 1, behind))
    last_ahead = piece(11, ACROSS, BEHIND2, 1, ahead)
    last_ahead.start()
    across_last.wait_send()
    for chunk in range(3):
        go(wo_across(chunk))
    docs_arrived(1, 1, 0)
    go(send_docs(4, 1, 0, 4, ahead))
    go(send_docs(5, 1, 0, 5, behind))
    docs_arrived(2, 0, 3)
    go(send_docs(6, 0, 3, 6, ahead))
    docs_arrived(3, 0, 1)
    go(remote(
        wo_ref.at[0], wo.at[0, pl.ds(pl.multiple_of(core * 256, 256), 256), :],
        wos_sem.at[2 * NW], wor_sem.at[2 * NW], twin,
    ))

    for copy in loads[3:]:
        copy.wait()
    remote(w.at[1 - core], w.at[1 - core], ws_sem.at[0], wr_sem.at[0], twin).wait_recv()
    kv_cols2 = w.at[2, :, pl.ds(pl.multiple_of((1 - core) * HD, HD), HD)]
    remote(kv_cols2, kv_cols2, ws_sem.at[1], wr_sem.at[1], twin).wait_recv()
    project(OWN, 2)
    docs_arrived(4, 1, 3)
    go(send_docs(7, 1, 3, 7, ahead))
    docs_arrived(5, 1, 1)
    def twin_keys(slots):
        for slot in slots:
            dh, dy = SLOTS[slot]
            ref = kv.at[PAD + 2 * block_of(dh, dy) + 1 - core]
            remote(ref, ref, kvs_sem.at[slot], kvr_sem.at[slot], twin).wait_recv()

    factor = HD ** (-0.5) * LOG2E

    def attend(dh, dy):
        block = 2 * block_of(dh, dy) + core
        heads = q[dh * YS + dy].reshape(4 * BLK, HD)
        keys = kv[pl.ds(block, WIN), :, :HD].reshape(WIN * BLK, HD)
        values = kv[pl.ds(block, WIN), :, HD:].reshape(WIN * BLK, HD)
        scores = lax.dot_general(
            heads, keys, (((1,), (1,)), ((), ())), preferred_element_type=jnp.float32
        ).reshape(4, BLK, WIN * BLK)
        key_docs = dc[pl.ds(block, WIN)].astype(jnp.float32)
        row_docs = jnp.broadcast_to(key_docs[WIN - 1], (BLK, BLK)).T
        tiles = []
        for index in range(WIN):
            same = row_docs == key_docs[index]
            if index == WIN - 1:
                same = same & (
                    lax.broadcasted_iota(jnp.int32, (BLK, BLK), 1)
                    <= lax.broadcasted_iota(jnp.int32, (BLK, BLK), 0)
                )
            tiles.append(
                jnp.where(same[None], scores[:, :, index * BLK : (index + 1) * BLK], -jnp.inf)
            )
        top = functools.reduce(jnp.maximum, tiles)
        top = jnp.max(top, axis=-1, keepdims=True) * factor
        tiles = [jnp.exp2(tile * factor - top) for tile in tiles]
        total = jnp.sum(functools.reduce(jnp.add, tiles), axis=-1, keepdims=True)
        probs = jnp.concatenate([tile.astype(jnp.bfloat16) for tile in tiles], axis=-1)
        res = jnp.dot(
            probs.reshape(4 * BLK, WIN * BLK), values, preferred_element_type=jnp.float32
        ).reshape(4, BLK, HD)
        return (res / total).astype(jnp.bfloat16)

    def att_copy(place):
        return remote(att.at[2, place], att.at[1, place], ats_sem.at[place], atr_sem.at[place], across)

    def attend_all(order):
        def one(i, carry):
            code = jnp.int32(order[-1])
            for index in range(len(order) - 1):
                code = jnp.where(i == index, order[index], code)
            dh, place = code // YS, code % YS
            dy = jnp.where(place < 2, 2 - place, 9 - 3 * place)
            res = attend(dh, dy)
            for head in range(4):
                att[2 * dh, place, :, head * HD : (head + 1) * HD] = res[head]

            @pl.when(dh == 1)
            def _():
                att_copy(place).start()

            return carry

        lax.fori_loop(0, len(order), one, 0)

    for slot in (BEHIND, AHEAD):
        for part in range(2):
            arrived(slot, part)
    go(wo_across(3))
    arrived(BEHIND2, 0)
    go(piece(12, BEHIND2, FAR2, 0, ahead))
    arrived(AHEAD2, 1)
    go(piece(13, AHEAD2, FAR2, 1, behind))
    last_ahead.wait_send()
    go(piece(6, BEHIND, FAR, 0, ahead))
    go(piece(7, AHEAD, FAR, 1, behind))
    go(wo_across(4))
    project(BEHIND, 2)
    pass_wo(0)
    arrived(BEHIND2, 1)
    arrived(AHEAD2, 0)
    project(BEHIND2, 2)
    pass_wo(1)
    docs_arrived(6, 0, 2)
    docs_arrived(7, 1, 2)
    arrived(FAR2, 0)
    arrived(FAR2, 1)
    project(FAR2, 1)
    twin_keys((OWN, ACROSS, BEHIND, AHEAD, BEHIND2, AHEAD2, FAR2))
    attend_all((4, 5, 1))
    pass_wo(2)
    pass_wo(3)
    arrived(FAR, 0)
    arrived(FAR, 1)
    project(FAR, 1)
    twin_keys((FAR,))
    attend_all((0,))
    pass_wo(4)
    own_wo = wo.at[0, pl.ds(pl.multiple_of((1 - core) * 256, 256), 256), :]
    remote(own_wo, own_wo, wos_sem.at[2 * NW], wor_sem.at[2 * NW], twin).wait_recv()
    att_copy(0).wait_recv()

    def half_copies(k):
        return (
            remote(far.at[k, FIRST, :], half_f.at[k], rs_send.at[0, k], rs_recv.at[0, k], ahead),
            remote(far.at[k, SECOND, :], half_b.at[k], rs_send.at[1, k], rs_recv.at[1, k], behind),
        )

    def full_copies(k):
        return (
            remote(fwd.at[k], got_f.at[k], rs_send.at[2, k], rs_recv.at[2, k], ahead),
            remote(bwd.at[k], got_b.at[k], rs_send.at[3, k], rs_recv.at[3, k], behind),
        )

    def cols(k):
        return pl.ds(pl.multiple_of(k * cw, cw), cw)

    def shift_copy(k):
        return remote(done.at[k], out_ref.at[0, :, cols(k)], sh_send.at[k], sh_recv.at[k], following)

    def product(first, count, k):
        return sum(
            jnp.dot(
                att[group, pl.ds(first, count)].reshape(count * BLK, 4 * HD),
                wo[group, :, cols(k)],
                preferred_element_type=jnp.float32,
            )
            for group in range(2)
        )

    def far_step(i, carry):
        for chunk in range(NW):
            @pl.when(i == chunk * (NJ // NW))
            def _():
                ref = wo.at[1, pl.ds(pl.multiple_of((1 - core) * 256, 256), 256), wo_piece(chunk)]
                remote(
                    ref, ref, wos_sem.at[NW + chunk], wor_sem.at[NW + chunk], twin
                ).wait_recv()

        far[i] = product(0, 1, i).astype(jnp.bfloat16)
        for copy in half_copies(i):
            copy.start()
        return carry

    lax.fori_loop(0, NJ, far_step, 0)
    attend_all((6, 7, 2, 3))
    att_copy(1).wait_recv()
    att_copy(2).wait_recv()

    def step(i, carry):
        @pl.when(i < NJ)
        def _():
            res = product(1, 2, i)
            first, second = half_copies(i)
            to_f, to_b = full_copies(i)
            first.wait_recv()
            fwd[i, SECOND, :] = res[HALF:BLK].astype(jnp.bfloat16)
            fwd[i, FIRST, :] = (res[:HALF] + half_f[i].astype(jnp.float32)).astype(jnp.bfloat16)
            to_f.start()
            second.wait_recv()
            bwd[i, FIRST, :] = res[BLK : BLK + HALF].astype(jnp.bfloat16)
            bwd[i, SECOND, :] = (res[BLK + HALF :] + half_b[i].astype(jnp.float32)).astype(jnp.bfloat16)
            to_b.start()

        @pl.when(i == LAG)
        def _():
            att_copy(3).wait_recv()

        @pl.when(i >= LAG)
        def _():
            k = i - LAG
            total = state[:, cols(k)].astype(jnp.float32) + product(3, 1, k)
            from_b, from_f = full_copies(k)
            from_b.wait_recv()
            from_f.wait_recv()
            total = total + got_f[k].astype(jnp.float32) + got_b[k].astype(jnp.float32)
            done[k] = total.astype(jnp.bfloat16)
            shift_copy(k).start()

        return carry

    lax.fori_loop(0, NJ + LAG, step, 0)

    for copy in sent:
        copy.wait_send()
    for place in range(YS):
        att_copy(place).wait_send()

    def finish(k, carry):
        for copy in half_copies(k) + full_copies(k):
            copy.wait_send()
        shift_copy(k).wait()
        return carry

    lax.fori_loop(0, NJ, finish, 0)
    remote(docs_ref, odocs_ref, dsend.at[9], drecv.at[9], following).wait_recv()


def local(state, docs, gain, w_query, w_keyval, w_out):
    width = state.shape[2]
    cw = width // NJ
    bf, f32 = jnp.bfloat16, jnp.float32
    dma = pltpu.SemaphoreType.DMA
    anyspace = pl.BlockSpec(memory_space=pl.ANY)
    return tuple(pl.pallas_call(
        body,
        out_shape=(
            jax.ShapeDtypeStruct(state.shape, state.dtype),
            jax.ShapeDtypeStruct(docs.shape, docs.dtype),
        ),
        in_specs=[anyspace] * 6,
        out_specs=(anyspace, anyspace),
        scratch_shapes=[
            pltpu.VMEM((BLK, width), bf),
            pltpu.VMEM((1, width), f32),
            pltpu.VMEM((8, BLK, width), bf),
            pltpu.VMEM((3, width, 2 * HD), bf),
            pltpu.VMEM((2, 4 * HD, width), bf),
            pltpu.VMEM((8, 4, BLK, HD), bf),
            pltpu.VMEM((16 + PAD, BLK, 2 * HD), bf),
            pltpu.VMEM((16 + PAD, 1, BLK), jnp.int32),
            pltpu.VMEM((3, YS, BLK, 4 * HD), bf),
            pltpu.VMEM((NJ, BLK, cw), bf),
            pltpu.VMEM((NJ, BLK, cw), bf),
            pltpu.VMEM((NJ, BLK, cw), bf),
            pltpu.VMEM((NJ, HALF, cw), bf),
            pltpu.VMEM((NJ, HALF, cw), bf),
            pltpu.VMEM((NJ, BLK, cw), bf),
            pltpu.VMEM((NJ, BLK, cw), bf),
            pltpu.VMEM((NJ, BLK, cw), bf),
            dma((6,)),
            dma((14,)), dma((8, 2)),
            dma((10,)), dma((10,)),
            dma((2,)), dma((2,)),
            dma((8,)), dma((8,)),
            dma((2 * NW + 1,)), dma((2 * NW + 1,)),
            dma((YS,)), dma((YS,)),
            dma((4, NJ)), dma((4, NJ)),
            dma((NJ,)), dma((NJ,)),
        ],
        compiler_params=pltpu.CompilerParams(
            collective_id=0, has_side_effects=True, vmem_limit_bytes=52 << 20
        ),
        name="layer",
    )(state, docs, gain, w_query, w_keyval, w_out))


def solution(mesh):
    in_specs = (
        P("section", "tensor", None),
        P("section", "tensor"),
        P("section", None),
        P("section", None, "tensor"),
        P("section", None, "tensor"),
        P("section", "tensor", None),
    )
    out_specs = (P("section", "tensor", None), P("section", "tensor"))
    return jax.shard_map(local, mesh=mesh, in_specs=in_specs, out_specs=out_specs, check_vma=False)
```
